32 devices in a mesh: cols: 16 (over z, y, x), walk: 2 (over core).
Axes of the slice: x: 2, y: 2, z: 4, core: 2. Of those that a mesh axis runs over, the one named last changes fastest.
Arguments:
- green_by_column: float32 [2, 4096, 4096], P('walk', 'cols'), parts along dimension 0, may hold values from -1.5 to 1.5
- field: int32 [2, 3, 4096], P('walk'), parts along dimension 0, may hold values from 0 to 1
Outputs:
- wrapped: float32 [2, 4096, 4096], P('walk', 'cols'), parts along dimension 0
The draws below stay inside these ranges and needn't reach their ends.
There are 2 independent parts, one for each index of `walk`. The reference program is written for one: setup_inputs(seed, part) draws one part's arguments, and reference() takes and returns one part's arrays. A program takes and returns all parts, laid end to end along the dimension named above; each array names one. Nothing has to cross between parts.
All inputs are finite; a program needn't handle non-finite values.
Results may differ from the reference program's by a relative error of at most 0.00012.
Values sent between devices are 32-bit elements; how exact they have to be, the bound alone decides.
No kernel may reach another device: no remote copies, remote signals or barrier semaphores. Data moves between devices by JAX's collectives and lax.ppermute only.
A program may use at most 64 MiB of HBM per device.

```python
import jax
import jax.numpy as jnp
from jax import lax

LX = 64
LY = 64
WALKERS = 1
SLICES = 3
SITES = 4096


def set_ends(entries, key, smallest, largest):
    shape = entries.shape
    index_at = [jax.random.randint(jax.random.fold_in(key, axis), (), 0, shape[axis]) for axis in range(len(shape))]
    entries = entries.at[tuple(index_at)].set(smallest)
    longest = shape.index(max(shape))
    index_at[longest] = (index_at[longest] + 1) % shape[longest]
    return entries.at[tuple(index_at)].set(largest)


def block_levels(stream_key, dims, pieces, least, top_value):
    def one(dim, blocks):
        heights = jax.random.uniform(jax.random.fold_in(jax.random.fold_in(stream_key, 6), dim), (blocks,), jnp.float32, least / len(pieces), top_value / len(pieces))
        return jnp.repeat(jnp.exp(heights), dims[dim] // blocks).reshape((-1,) + (1,) * (len(dims) - dim - 1))

    level = one(*pieces[0])
    for cut in pieces[1:]:
        level = level * one(*cut)
    return level


def gaussian(stream_key, extent, scale, most, split=(), dtype=jnp.bfloat16):
    drawn = scale * jax.random.normal(stream_key, extent, jnp.float32)
    if split:
        drawn = drawn * block_levels(stream_key, extent, split, -0.22, 0.18)
    return jnp.clip(drawn, -most, most).astype(dtype)


def setup_inputs(seed: int = 0, part: int = 0) -> dict:
    key_list = jax.random.split(jax.random.key(seed), 3)
    own_keys = jax.random.split(jax.random.fold_in(key_list[2], part), 3)
    return {
        "green_by_column": gaussian(own_keys[0], (WALKERS, SITES, SITES), 0.25, 1.5, ((1, 16),), jnp.float32),
        "field": set_ends(jax.random.randint(own_keys[1], (WALKERS, SLICES, SITES), 0, 2), jax.random.fold_in(own_keys[1], 1), 0, 1).astype(jnp.int32),
    }


hop_rate = 0.6
coupling = 0.65373


def kernel(length, growth):
    indices = jnp.arange(length)
    spectrum = jnp.exp(growth * jnp.cos(2.0 * jnp.pi * indices.astype(jnp.float32) / length))
    column = jnp.fft.ifft(spectrum).real.astype(jnp.float32)
    differ = (indices[:, None] - indices[None, :]) % length
    return column[differ]


def reference(green_by_column, field):
    fwd_x = kernel(LX, hop_rate)
    fwd_y = kernel(LY, hop_rate)
    inv_x = kernel(LX, -hop_rate)
    inv_y = kernel(LY, -hop_rate)
    spins = 2.0 * field.astype(jnp.float32) - 1.0
    highest = lax.Precision.HIGHEST

    def advance(inputs_pair):
        green, spin_rows = inputs_pair
        for moment in range(SLICES):
            boost = jnp.exp(coupling * spin_rows[moment])
            green = green * boost[None, :] / boost[:, None]
            blocks = green.reshape(SITES, LX, LY)
            blocks = jnp.einsum("xa,jab->jxb", fwd_x, blocks, precision=highest)
            blocks = jnp.einsum("yb,jxb->jxy", fwd_y, blocks, precision=highest)
            blocks = blocks.reshape(LX, LY, SITES)
            blocks = jnp.einsum("ax,abi->xbi", inv_x, blocks, precision=highest)
            blocks = jnp.einsum("by,xbi->xyi", inv_y, blocks, precision=highest)
            green = blocks.reshape(SITES, SITES)
        return green

    return lax.map(advance, (green_by_column, spins))
```

```python
import functools
import jax
import jax.numpy as jnp
import ml_dtypes
import numpy as np
from jax import lax
from jax.experimental import pallas as pl
from jax.experimental.pallas import tpu as pltpu
from jax.sharding import PartitionSpec as P

LX = 64
LY = 64
SLICES = 3
hop_rate = 0.6
coupling = 0.65373
LANES = 128
TALL = 256
UNROLL = 8
BF = jnp.bfloat16
F32 = jnp.float32


def circulant(length, growth):
    angles = 2.0 * np.pi * np.arange(length) / length
    column = np.cos(np.outer(np.arange(length), angles)) @ np.exp(growth * np.cos(angles)) / length
    differ = (np.arange(length)[:, None] - np.arange(length)[None, :]) % length
    return column[differ]


def split_matrix(matrix):
    high = matrix.astype(ml_dtypes.bfloat16)
    return high, (matrix - high.astype(np.float64)).astype(ml_dtypes.bfloat16)


def lane_side(matrix):
    high, low = split_matrix(np.kron(np.eye(LANES // matrix.shape[0]), matrix).T)
    return jnp.asarray(np.tile(np.concatenate([high, low], axis=1), (2, 1)))


def row_side(matrix):
    high, low = split_matrix(np.kron(np.eye(LANES // matrix.shape[0]), matrix))
    return jnp.asarray(np.tile(np.concatenate([high, low], axis=0), (1, 2)))


def halves(value):
    high = value.astype(BF)
    return high, (value - high.astype(F32)).astype(BF)


def mix_lanes(data, right):
    high, low = halves(data)
    both = jnp.dot(jnp.concatenate([high, low], axis=1), right, preferred_element_type=F32)
    return both[:, :LANES] + both[:, LANES:]


def mix_rows(left, data):
    high, low = halves(data)
    mid = data.shape[0] // 2
    stacked = jnp.concatenate(
        [jnp.concatenate([part[:mid], part[mid:]], axis=1) for part in (high, low)], axis=0
    )
    both = jnp.dot(left, stacked, preferred_element_type=F32)
    both = both[:mid] + both[mid:]
    return jnp.concatenate([both[:, :LANES], both[:, LANES:]], axis=0)


def swap_halves(first, second):
    low = lax.broadcasted_iota(jnp.int32, first.shape, 1) < LANES // 2
    return (
        jnp.where(low, first, pltpu.roll(second, LANES // 2, 1)),
        jnp.where(low, pltpu.roll(first, LANES // 2, 1), second),
    )


def left_body(parts, joined, me_ref, x_ref, gain_ref, right_ref, left_ref, *rest):
    outs, work = rest[:-1], rest[-1]
    rows = x_ref.shape[0]
    me = me_ref[0]
    pairs = LX // 2
    for group in range(rows // 16):
        for c in range(pairs):
            lanes = slice(c * LANES, (c + 1) * LANES)
            even, odd = swap_halves(x_ref[group * 16 : group * 16 + 8, lanes], x_ref[group * 16 + 8 : group * 16 + 16, lanes])
            work[pl.ds(group * 8 * LX + 2 * c, 8, stride=LX), :] = even
            work[pl.ds(group * 8 * LX + 2 * c + 1, 8, stride=LX), :] = odd
    tall = left_ref.shape[1]
    for moment in range(SLICES):
        gain = gain_ref[moment]
        gain = jnp.concatenate([gain] * (tall // LX), axis=0)

        @pl.loop(0, work.shape[0] // tall // UNROLL)
        def _(step):
            for q in range(UNROLL):
                at = pl.ds(pl.multiple_of((step * UNROLL + q) * tall, tall), tall)
                work[at, :] = mix_lanes(work[at, :] * gain, right_ref[...])

        @pl.loop(0, work.shape[0] // tall // UNROLL)
        def _(step):
            for q in range(UNROLL):
                at = pl.ds(pl.multiple_of((step * UNROLL + q) * tall, tall), tall)
                work[at, :] = mix_rows(left_ref[...], work[at, :])

    blocks = LX // parts
    for mask in range(parts):
        start = (me ^ mask) * blocks
        for half in range(blocks // 2):
            for group in range(rows // 16):
                even = work[pl.ds(group * 8 * LX + start + 2 * half, 8, stride=LX), :]
                odd = work[pl.ds(group * 8 * LX + start + 2 * half + 1, 8, stride=LX), :]
                first, second = swap_halves(even, odd)
                if joined:
                    ref, lanes = outs[mask], slice(half * LANES, (half + 1) * LANES)
                else:
                    ref, lanes = outs[half * parts + mask], slice(0, LANES)
                ref[group * 16 : group * 16 + 8, lanes] = first
                ref[group * 16 + 8 : group * 16 + 16, lanes] = second


def left_chain(parts, block, first, steps, joined, me, x, gain, right, left):
    sites = x.shape[1]
    halves_ = sites // parts // LANES
    if joined:
        out_shape = [jax.ShapeDtypeStruct((steps * block, sites // parts), F32)] * parts
        out_specs = [pl.BlockSpec((block, sites // parts), lambda g: (g, 0))] * parts
    else:
        out_shape = [jax.ShapeDtypeStruct((steps * block, LANES), F32)] * (parts * halves_)
        out_specs = [pl.BlockSpec((block, LANES), lambda g: (g, 0))] * (parts * halves_)
    whole = lambda array: pl.BlockSpec(array.shape, lambda g: (0,) * array.ndim)
    return pl.pallas_call(
        functools.partial(left_body, parts, joined),
        grid=(steps,),
        in_specs=[
            pl.BlockSpec(memory_space=pltpu.SMEM),
            pl.BlockSpec((block, sites), lambda g: (g + first, 0)),
            whole(gain), whole(right), whole(left),
        ],
        out_specs=out_specs,
        out_shape=out_shape,
        scratch_shapes=[pltpu.VMEM((block // 2 * LX, LANES), F32)],
        compiler_params=pltpu.CompilerParams(vmem_limit_bytes=32 << 20),
        cost_estimate=pl.CostEstimate(flops=steps * block * sites * 256 * 2 * 6, bytes_accessed=steps * block * sites * 8, transcendentals=0),
    )(me, x, gain, right, left)


def right_body(parts, counts, me_ref, loss_ref, left_y_ref, left_x_ref, *rest):
    n = len(counts)
    ins, outs, work = rest[: parts * n], rest[parts * n : parts * n + parts], rest[-1]
    me = me_ref[0]
    sites = work.shape[0]
    local = sites // parts
    for mask in range(parts):
        top = (me ^ mask) * local
        for count, ref, lane in [(counts[q][0], ins[q * parts + mask], counts[q][1]) for q in range(n)]:
            work[pl.ds(pl.multiple_of(top, local), count), :] = ref[:, lane : lane + LANES]
            top = top + count
    tall = left_y_ref.shape[1]
    step = tall // LX
    for moment in range(SLICES):

        @pl.loop(0, sites // tall // UNROLL)
        def _(turn):
            for q in range(UNROLL):
                at = pl.ds(pl.multiple_of((turn * UNROLL + q) * tall, tall), tall)
                work[at, :] = mix_rows(left_y_ref[...], work[at, :] * loss_ref[moment, at, :])

        @pl.loop(0, LY // step // UNROLL)
        def _(turn):
            for r in range(UNROLL):
                y = (turn * UNROLL + r) * step
                data = jnp.concatenate([work[pl.ds(y + q, LX, stride=LY), :] for q in range(step)], axis=0)
                data = mix_rows(left_x_ref[...], data)
                for q in range(step):
                    work[pl.ds(y + q, LX, stride=LY), :] = data[q * LX : (q + 1) * LX]

    for mask in range(parts):
        outs[mask][...] = work[pl.ds(pl.multiple_of((me ^ mask) * local, local), local), :]


def right_chain(parts, counts, me, loss, left_y, left_x, pieces):
    sites = loss.shape[1]
    local = sites // parts
    whole = pl.BlockSpec(memory_space=pltpu.VMEM)
    return pl.pallas_call(
        functools.partial(right_body, parts, counts),
        in_specs=[pl.BlockSpec(memory_space=pltpu.SMEM)] + [whole] * (3 + len(pieces)),
        out_specs=[whole] * parts,
        out_shape=[jax.ShapeDtypeStruct((local, LANES), F32)] * parts,
        scratch_shapes=[pltpu.VMEM((sites, LANES), F32)],
        compiler_params=pltpu.CompilerParams(vmem_limit_bytes=40 << 20),
        cost_estimate=pl.CostEstimate(flops=sites * LANES * 256 * 2 * 6, bytes_accessed=sites * LANES * 8 + loss.size * 4, transcendentals=0),
    )(me, loss, left_y, left_x, *pieces)


def kernel(length, growth):
    indices = jnp.arange(length, dtype=jnp.int32)
    phases = indices[:, None] * indices[None, :] % length
    angles = 2.0 * jnp.pi * phases.astype(jnp.float32) / length
    cosines = jnp.cos(angles)
    sines = jnp.sin(angles)
    spectrum = jnp.exp(growth * jnp.cos(2.0 * jnp.pi * indices.astype(jnp.float32) / length))
    highest = lax.Precision.HIGHEST
    total = jnp.dot(cosines * spectrum[None, :], cosines.T, precision=highest)
    total = total + jnp.dot(sines * spectrum[None, :], sines.T, precision=highest)
    return total / length


def whole_exchange(green_by_column, field):
    highest = lax.Precision.HIGHEST
    walkers, local_cols, sites = green_by_column.shape
    fwd_x = kernel(LX, hop_rate)
    fwd_y = kernel(LY, hop_rate)
    inv_x = kernel(LX, -hop_rate)
    inv_y = kernel(LY, -hop_rate)
    spins = 2.0 * field.astype(jnp.float32) - 1.0
    green = green_by_column
    for moment in range(SLICES):
        left_green = green
        left_green = left_green * jnp.exp(coupling * spins[:, moment, :])[:, None, :]
        left_blocks = left_green.reshape(walkers, local_cols, LX, LY)
        left_blocks = jnp.einsum("xa,wcab->wcxb", fwd_x, left_blocks, precision=highest)
        left_blocks = jnp.einsum("yb,wcxb->wcxy", fwd_y, left_blocks, precision=highest)
        green = left_blocks.reshape(walkers, local_cols, sites)
    parts = lax.axis_size("cols")
    shaped_in = green.reshape(walkers, local_cols, parts, sites // parts)
    row_block = lax.all_to_all(shaped_in, "cols", split_axis=2, concat_axis=1, tiled=True)
    count = row_block.shape[0]
    width = row_block.shape[3]
    blocks = row_block.reshape(count, sites, width)
    for moment in range(SLICES):
        blocks = blocks * jnp.exp(-coupling * spins[:, moment, :])[:, :, None]
        shaped = blocks.reshape(count, LX, LY, width)
        shaped = jnp.einsum("by,wabr->wayr", inv_y, shaped, precision=highest)
        shaped = jnp.einsum("ax,wayr->wxyr", inv_x, shaped, precision=highest)
        blocks = shaped.reshape(count, sites, width)
    rows_done = blocks.reshape(count, sites, 1, width)
    rows_done = rows_done.reshape(walkers, sites, sites // parts)
    green = lax.all_to_all(rows_done, "cols", split_axis=1, concat_axis=2, tiled=True)
    return green


def send_order(parts):
    far = [m for pair in zip(range(3 * parts // 4, parts), range(parts // 2, 3 * parts // 4)) for m in pair]
    near = [m for pair in zip(range(parts // 4, parts // 2), range(1, parts // 4 + 1)) for m in pair][: parts // 2 - 1]
    order = []
    for at in range(0, parts // 2, 2):
        order += far[at : at + 2] + near[at : at + 2]
    return order


def exchange(blocks, parts):
    received = [blocks[0]] + [None] * (parts - 1)
    for mask in send_order(parts):
        received[mask] = lax.ppermute(blocks[mask], "cols", [(s, s ^ mask) for s in range(parts)])
    return received


def pipelined(green_by_column, field):
    _, rows, sites = green_by_column.shape
    parts = lax.axis_size("cols")
    local = sites // parts
    me = lax.axis_index("cols").astype(jnp.int32)
    at = me.reshape(1)
    x = green_by_column.reshape(rows, sites)
    spins = 2.0 * field.reshape(SLICES, sites).astype(F32) - 1.0
    gain = jnp.exp(coupling * spins).reshape(SLICES, LX, LY)
    gain = jnp.concatenate([gain] * (LANES // LY), axis=2)
    loss = jnp.broadcast_to(jnp.exp(-coupling * spins)[:, :, None], (SLICES, sites, LANES))
    right = lane_side(circulant(LY, hop_rate))
    left = row_side(circulant(LX, hop_rate))
    left_y = row_side(circulant(LY, -hop_rate))
    left_x = row_side(circulant(LX, -hop_rate))
    block = rows // 4
    early = left_chain(parts, block, 0, 1, True, at, x, gain, right, left)
    late = left_chain(parts, block, 1, 3, False, at, x, gain, right, left)
    early = exchange(early, parts)
    result = jnp.zeros((rows, sites), F32)
    late = [exchange(late[h * parts : (h + 1) * parts], parts) for h in range(local // LANES)]
    for h, pieces in enumerate(late):
        counts = ((block, h * LANES), (rows - block, 0))
        done = exchange(right_chain(parts, counts, at, loss, left_y, left_x, early + pieces), parts)
        for mask in [0] + send_order(parts):
            result = lax.dynamic_update_slice(result, done[mask], (0, (me ^ mask) * local + h * LANES))
    return result.reshape(green_by_column.shape)


def shards(green_by_column, field):
    walkers, rows, sites = green_by_column.shape
    parts = lax.axis_size("cols")
    fits = walkers == 1 and rows == 256 and rows * parts == sites and parts & (parts - 1) == 0 and parts >= 8
    if fits and LX * LY == sites and LX == LY == 64:
        return pipelined(green_by_column, field)
    return whole_exchange(green_by_column, field)


def solution(mesh):
    return jax.shard_map(
        shards,
        mesh=mesh,
        in_specs=(P("walk", "cols", None), P("walk", None, None)),
        out_specs=P("walk", "cols", None),
        check_vma=False,
    )
```

```python
import functools
import jax
import jax.numpy as jnp
import ml_dtypes
import numpy as np
from jax import lax
from jax.experimental import pallas as pl
from jax.experimental.pallas import tpu as pltpu
from jax.sharding import PartitionSpec as P

LX = 64
LY = 64
SLICES = 3
hop_rate = 0.6
coupling = 0.65373
LANES = 128
TALL = 256
UNROLL = 8
VMEM_LIMIT = 60 << 20
IN_FLIGHT = 5
AHEAD = 5
LATE = 5
BF = jnp.bfloat16
F32 = jnp.float32


def circulant(length, growth):
    angles = 2.0 * np.pi * np.arange(length) / length
    column = np.cos(np.outer(np.arange(length), angles)) @ np.exp(growth * np.cos(angles)) / length
    differ = (np.arange(length)[:, None] - np.arange(length)[None, :]) % length
    return column[differ]


def split_matrix(matrix):
    high = matrix.astype(ml_dtypes.bfloat16)
    return high, (matrix - high.astype(np.float64)).astype(ml_dtypes.bfloat16)


def lane_side(matrix):
    high, low = split_matrix(np.kron(np.eye(LANES // matrix.shape[0]), matrix).T)
    return jnp.asarray(np.tile(np.concatenate([high, low], axis=1), (2, 1)))


def row_side(matrix):
    high, low = split_matrix(np.kron(np.eye(LANES // matrix.shape[0]), matrix))
    return jnp.asarray(np.tile(np.concatenate([high, low], axis=0), (1, 2)))


def halves(value):
    high = value.astype(BF)
    return high, (value - high.astype(F32)).astype(BF)


def mix_lanes(data, right):
    high, low = halves(data)
    both = jnp.dot(jnp.concatenate([high, low], axis=1), right, preferred_element_type=F32)
    return both[:, :LANES] + both[:, LANES:]


def mix_rows(left, data):
    high, low = halves(data)
    mid = data.shape[0] // 2
    stacked = jnp.concatenate(
        [jnp.concatenate([part[:mid], part[mid:]], axis=1) for part in (high, low)], axis=0
    )
    both = jnp.dot(left, stacked, preferred_element_type=F32)
    both = both[:mid] + both[mid:]
    return jnp.concatenate([both[:, :LANES], both[:, LANES:]], axis=0)


def swap_halves(first, second):
    low = lax.broadcasted_iota(jnp.int32, first.shape, 1) < LANES // 2
    return (
        jnp.where(low, first, pltpu.roll(second, LANES // 2, 1)),
        jnp.where(low, pltpu.roll(first, LANES // 2, 1), second),
    )


def partner(parts, mask):
    return lax.axis_index("cols").astype(jnp.int32) ^ mask


def left_body(parts, x_ref, field_ref, right_ref, left_ref, *rest):
    outs, gain_ref, work = rest[:-2], rest[-2], rest[-1]
    rows = x_ref.shape[0]

    @pl.when(pl.program_id(0) == 0)
    def _():
        gain = [jnp.exp(coupling * (2.0 * field_ref[moment].astype(F32) - 1.0)) for moment in range(SLICES)]
        for moment in range(SLICES):
            for c in range(LX // 2):
                row = jnp.broadcast_to(gain[moment][:, c * LANES : (c + 1) * LANES], (8, LANES))
                even, odd = swap_halves(row, row)
                gain_ref[moment, 2 * c : 2 * c + 1, :] = even[:1]
                gain_ref[moment, 2 * c + 1 : 2 * c + 2, :] = odd[:1]

    for group in range(rows // 16):
        for c in range(LX // 2):
            lanes = slice(c * LANES, (c + 1) * LANES)
            even, odd = swap_halves(x_ref[group * 16 : group * 16 + 8, lanes], x_ref[group * 16 + 8 : group * 16 + 16, lanes])
            work[pl.ds(group * 8 * LX + 2 * c, 8, stride=LX), :] = even
            work[pl.ds(group * 8 * LX + 2 * c + 1, 8, stride=LX), :] = odd
    for moment in range(SLICES):
        gain = jnp.concatenate([gain_ref[moment]] * (TALL // LX), axis=0)
        for top in range(0, work.shape[0], TALL):
            work[top : top + TALL, :] = mix_lanes(work[top : top + TALL, :] * gain, right_ref[...])
        for top in range(0, work.shape[0], TALL):
            work[top : top + TALL, :] = mix_rows(left_ref[...], work[top : top + TALL, :])
    far = parts // 2
    for mask in range(parts):
        for half in range(2):
            ref = outs[mask if mask < far else half * far + mask]
            lanes = slice(half * LANES, (half + 1) * LANES) if mask < far else slice(0, LANES)
            start = partner(parts, mask) * (LX // parts) + 2 * half
            for group in range(rows // 16):
                even = work[pl.ds(group * 8 * LX + start, 8, stride=LX), :]
                odd = work[pl.ds(group * 8 * LX + start + 1, 8, stride=LX), :]
                above, below = swap_halves(even, odd)
                ref[group * 16 : group * 16 + 8, lanes] = above
                ref[group * 16 + 8 : group * 16 + 16, lanes] = below


def left_chain(parts, block, x, field, right, left):
    rows, sites = x.shape
    far = parts // 2
    widths = [2 * LANES] * far + [LANES] * parts
    whole = lambda array: pl.BlockSpec(array.shape, lambda g: (0,) * array.ndim)
    outs = pl.pallas_call(
        functools.partial(left_body, parts),
        grid=(rows // block,),
        in_specs=[pl.BlockSpec((block, sites), lambda g: (g, 0)), whole(field), whole(right), whole(left)],
        out_specs=[pl.BlockSpec((block, width), lambda g: (g, 0)) for width in widths],
        out_shape=[jax.ShapeDtypeStruct((rows, width), F32) for width in widths],
        scratch_shapes=[pltpu.VMEM((SLICES, LX, LANES), F32), pltpu.VMEM((block // 2 * LX, LANES), F32)],
        compiler_params=pltpu.CompilerParams(vmem_limit_bytes=VMEM_LIMIT),
        cost_estimate=pl.CostEstimate(flops=rows * sites * 256 * 2 * 6, bytes_accessed=rows * sites * 8, transcendentals=0),
        name="left_chain",
    )(x, field, right, left)
    return outs[:far], outs[far:parts], outs[parts:]


def right_body(parts, joined, loss_ref, left_y_ref, left_x_ref, *rest):
    pieces, outs, work = rest[:parts], rest[-parts - 1 : -1], rest[-1]
    sites = work.shape[0]
    local = sites // parts

    def rows_of(mask):
        return pl.ds(pl.multiple_of(partner(parts, mask) * local, local), local)

    for mask in range(parts):
        work[rows_of(mask), :] = pieces[mask][...]
    step = TALL // LX
    for moment in range(SLICES):

        @pl.loop(0, sites // TALL // UNROLL)
        def _(turn):
            for q in range(UNROLL):
                at = pl.ds(pl.multiple_of((turn * UNROLL + q) * TALL, TALL), TALL)
                work[at, :] = mix_rows(left_y_ref[...], work[at, :] * loss_ref[at, moment : moment + 1])

        @pl.loop(0, LY // step // UNROLL)
        def _(turn):
            for r in range(UNROLL):
                y = (turn * UNROLL + r) * step
                data = jnp.concatenate([work[pl.ds(y + q, LX, stride=LY), :] for q in range(step)], axis=0)
                data = mix_rows(left_x_ref[...], data)
                for q in range(step):
                    work[pl.ds(y + q, LX, stride=LY), :] = data[q * LX : (q + 1) * LX]

    for mask in range(parts):
        if joined and mask < parts // 2:
            outs[mask][:, :LANES] = rest[parts + mask][...]
            outs[mask][:, LANES:] = work[rows_of(mask), :]
        else:
            outs[mask][...] = work[rows_of(mask), :]


def right_chain(parts, half, loss, left_y, left_x, pieces, before=()):
    sites = loss.shape[0]
    rows = pieces[0].shape[0]
    widths = [LANES * 2 if before and mask < parts // 2 else LANES for mask in range(parts)]
    lane = lambda array: half if array.shape[1] > LANES else 0
    whole = lambda array: pl.BlockSpec(array.shape, lambda g: (0,) * array.ndim)
    return pl.pallas_call(
        functools.partial(right_body, parts, bool(before)),
        grid=(1,),
        in_specs=[whole(loss), whole(left_y), whole(left_x)]
        + [pl.BlockSpec((rows, LANES), functools.partial(lambda at, g: (0, at), lane(piece))) for piece in pieces]
        + [whole(array) for array in before],
        out_specs=[pl.BlockSpec((rows, width), lambda g: (0, 0)) for width in widths],
        out_shape=[jax.ShapeDtypeStruct((rows, width), F32) for width in widths],
        scratch_shapes=[pltpu.VMEM((sites, LANES), F32)],
        compiler_params=pltpu.CompilerParams(vmem_limit_bytes=VMEM_LIMIT),
        cost_estimate=pl.CostEstimate(flops=sites * LANES * 256 * 2 * 6, bytes_accessed=sites * LANES * 12, transcendentals=0),
        name="right_chain",
    )(loss, left_y, left_x, *pieces, *before)


def place_body(parts, spots, held, *rest):
    count = len(spots)
    blocks, out, landed, came, went = rest[:count], rest[count + held], rest[-3], rest[-2], rest[-1]
    local = out.shape[1] // parts
    copies = []
    column = 0
    for at, (mask, lane) in enumerate(spots):
        width = blocks[at].shape[1]
        spot = landed.at[:, pl.ds(column, width)]
        column += width
        start = pl.multiple_of(partner(parts, mask) * local + lane, LANES)
        copies.append((
            pltpu.make_async_copy(blocks[at], spot, came.at[at]),
            pltpu.make_async_copy(spot, out.at[:, pl.ds(start, width)], went.at[at]),
        ))
    for copy, _ in copies:
        copy.start()
    for copy, onward in copies:
        copy.wait()
        onward.start()
    for _, onward in copies:
        onward.wait()


def place(parts, spots, blocks, held=None):
    rows = blocks[0].shape[0]
    width = sum(block.shape[1] for block in blocks)
    held = [] if held is None else [held]
    anywhere = pl.BlockSpec(memory_space=pl.ANY)
    return pl.pallas_call(
        functools.partial(place_body, parts, spots, len(held)),
        in_specs=[anywhere] * (len(blocks) + len(held)),
        out_specs=anywhere,
        out_shape=jax.ShapeDtypeStruct((rows, rows * parts), F32),
        scratch_shapes=[pltpu.VMEM((rows, width), F32)] + [pltpu.SemaphoreType.DMA((len(blocks),))] * 2,
        input_output_aliases={len(blocks): 0} if held else {},
        compiler_params=pltpu.CompilerParams(vmem_limit_bytes=VMEM_LIMIT),
        cost_estimate=pl.CostEstimate(flops=0, bytes_accessed=rows * width * 8, transcendentals=0),
        name="place",
    )(*blocks, *held)


def kernel(length, growth):
    indices = jnp.arange(length, dtype=jnp.int32)
    phases = indices[:, None] * indices[None, :] % length
    angles = 2.0 * jnp.pi * phases.astype(jnp.float32) / length
    cosines = jnp.cos(angles)
    sines = jnp.sin(angles)
    spectrum = jnp.exp(growth * jnp.cos(2.0 * jnp.pi * indices.astype(jnp.float32) / length))
    highest = lax.Precision.HIGHEST
    total = jnp.dot(cosines * spectrum[None, :], cosines.T, precision=highest)
    total = total + jnp.dot(sines * spectrum[None, :], sines.T, precision=highest)
    return total / length


def whole_exchange(green_by_column, field):
    highest = lax.Precision.HIGHEST
    walkers, local_cols, sites = green_by_column.shape
    fwd_x = kernel(LX, hop_rate)
    fwd_y = kernel(LY, hop_rate)
    inv_x = kernel(LX, -hop_rate)
    inv_y = kernel(LY, -hop_rate)
    spins = 2.0 * field.astype(jnp.float32) - 1.0
    green = green_by_column
    for moment in range(SLICES):
        left_green = green
        left_green = left_green * jnp.exp(coupling * spins[:, moment, :])[:, None, :]
        left_blocks = left_green.reshape(walkers, local_cols, LX, LY)
        left_blocks = jnp.einsum("xa,wcab->wcxb", fwd_x, left_blocks, precision=highest)
        left_blocks = jnp.einsum("yb,wcxb->wcxy", fwd_y, left_blocks, precision=highest)
        green = left_blocks.reshape(walkers, local_cols, sites)
    parts = lax.axis_size("cols")
    shaped_in = green.reshape(walkers, local_cols, parts, sites // parts)
    row_block = lax.all_to_all(shaped_in, "cols", split_axis=2, concat_axis=1, tiled=True)
    count = row_block.shape[0]
    width = row_block.shape[3]
    blocks = row_block.reshape(count, sites, width)
    for moment in range(SLICES):
        blocks = blocks * jnp.exp(-coupling * spins[:, moment, :])[:, :, None]
        shaped = blocks.reshape(count, LX, LY, width)
        shaped = jnp.einsum("by,wabr->wayr", inv_y, shaped, precision=highest)
        shaped = jnp.einsum("ax,wayr->wxyr", inv_x, shaped, precision=highest)
        blocks = shaped.reshape(count, sites, width)
    rows_done = blocks.reshape(count, sites, 1, width)
    rows_done = rows_done.reshape(walkers, sites, sites // parts)
    green = lax.all_to_all(rows_done, "cols", split_axis=1, concat_axis=2, tiled=True)
    return green


class Links:
    def __init__(self, parts):
        self.parts = parts
        self.sent = []
        self.after = None

    def send(self, block, mask):
        hold = [self.after] if self.after is not None else []
        back = len(self.sent) - IN_FLIGHT
        if back >= 0:
            hold.append(self.sent[back]["value"])
        if hold:
            got = lax.optimization_barrier(tuple([block] + hold))
            block = got[0]
            if back >= 0:
                self.sent[back]["value"] = got[-1]
        value = lax.ppermute(block, "cols", [(s, s ^ mask) for s in range(self.parts)])
        self.sent.append({"value": value})
        return self.sent[-1]


def woven(first, second):
    pairs = [(first[at : at + 1], second[at : at + 1]) for at in range(max(len(first), len(second)))]
    return [mask for pair in pairs for part in pair for mask in part]


def pipelined(green_by_column, field):
    _, rows, sites = green_by_column.shape
    parts = lax.axis_size("cols")
    half = parts // 2
    x = green_by_column.reshape(rows, sites)
    loss = jnp.exp(-coupling * (2.0 * field[0].astype(F32) - 1.0)).T
    right = lane_side(circulant(LY, hop_rate))
    left = row_side(circulant(LX, hop_rate))
    left_y = row_side(circulant(LY, -hop_rate))
    left_x = row_side(circulant(LX, -hop_rate))
    far = [m for pair in zip(range(3 * parts // 4, parts), range(half, 3 * parts // 4)) for m in pair]
    near = [m for pair in zip(range(parts // 4, half), range(1, parts // 4 + 1)) for m in pair][: half - 1]
    every = range(half, parts)
    links = Links(parts)

    def chain(h, near_held, far_held, before=()):
        pieces = [near_held[m]["value"] for m in range(half)] + [far_held[m]["value"] for m in every]
        outs = right_chain(parts, h, loss, left_y, left_x, pieces, before)
        links.after = outs[0]
        return outs

    near_blocks, *far_blocks = left_chain(parts, rows // 4, x, field.transpose(1, 0, 2), right, left)
    near_held = {0: {"value": near_blocks[0]}}
    far_held = [{}, {}]
    for mask in woven(far, near):
        if mask < half:
            near_held[mask] = links.send(near_blocks[mask], mask)
        else:
            far_held[0][mask] = links.send(far_blocks[0][mask - half], mask)
    for at, mask in enumerate(far):
        if at == LATE:
            early = chain(0, near_held, far_held[0])
        far_held[1][mask] = links.send(far_blocks[1][mask - half], mask)
    far_done = [{}, {}]
    for at, mask in enumerate(far):
        if at == AHEAD:
            late = chain(1, near_held, far_held[1], early[:half])
        far_done[0][mask] = links.send(early[mask], mask)
    near_done = {0: {"value": late[0]}}
    for mask in woven(far, near):
        if mask < half:
            near_done[mask] = links.send(late[mask], mask)
        else:
            far_done[1][mask] = links.send(late[mask], mask)
    result = place(parts, [(m, 0) for m in every], [far_done[0][m]["value"] for m in every])
    spots = [(m, 0) for m in range(half)] + [(m, LANES) for m in every]
    blocks = [near_done[m]["value"] for m in range(half)] + [far_done[1][m]["value"] for m in every]
    return place(parts, spots, blocks, result).reshape(green_by_column.shape)


def shards(green_by_column, field):
    walkers, rows, sites = green_by_column.shape
    parts = lax.axis_size("cols")
    fits = walkers == 1 and rows == 256 and rows * parts == sites and parts & (parts - 1) == 0 and parts >= 8
    if fits and LX * LY == sites and LX == LY == 64:
        return pipelined(green_by_column, field)
    return whole_exchange(green_by_column, field)


def solution(mesh):
    return jax.shard_map(
        shards,
        mesh=mesh,
        in_specs=(P("walk", "cols", None), P("walk", None, None)),
        out_specs=P("walk", "cols", None),
        check_vma=False,
    )
```

```python
import functools
import jax
import jax.numpy as jnp
import ml_dtypes
import numpy as np
from jax import lax
from jax.experimental import pallas as pl
from jax.experimental.pallas import tpu as pltpu
from jax.sharding import PartitionSpec as P

LX = 64
LY = 64
SLICES = 3
hop_rate = 0.6
coupling = 0.65373
LANES = 128
TALL = 256
ROW_PAD = 8
PAIR_PAD = 8
UNROLL = 8
VMEM_LIMIT = 60 << 20
RIGHT_LIMIT = 24 << 20
IN_FLIGHT = 5
PATTERNS = ('nfnfnfnfnfnfnff', 'fnfnfnfnfnfnfnf', 'fnfnfnfnfnfnfnf', 'nfnfnfnfnfnfnff')
LATE = 5
AHEAD = 5
BF = jnp.bfloat16
F32 = jnp.float32


def circulant(length, growth):
    angles = 2.0 * np.pi * np.arange(length) / length
    column = np.cos(np.outer(np.arange(length), angles)) @ np.exp(growth * np.cos(angles)) / length
    differ = (np.arange(length)[:, None] - np.arange(length)[None, :]) % length
    return column[differ]


def split_matrix(matrix):
    high = matrix.astype(ml_dtypes.bfloat16)
    return high, (matrix - high.astype(np.float64)).astype(ml_dtypes.bfloat16)


def lane_side(matrix):
    high, low = split_matrix(np.kron(np.eye(LANES // matrix.shape[0]), matrix).T)
    return jnp.asarray(np.tile(np.concatenate([high, low], axis=1), (2, 1)))


def row_side(matrix):
    high, low = split_matrix(np.kron(np.eye(LANES // matrix.shape[0]), matrix))
    return jnp.asarray(np.tile(np.concatenate([high, low], axis=0), (1, 2)))


def halves(value):
    high = value.astype(BF)
    return high, (value - high.astype(F32)).astype(BF)


def mix_lanes(data, right):
    high, low = halves(data)
    both = jnp.dot(jnp.concatenate([high, low], axis=1), right, preferred_element_type=F32)
    return both[:, :LANES] + both[:, LANES:]


def mix_rows(left, data):
    high, low = halves(data)
    mid = data.shape[0] // 2
    stacked = jnp.concatenate(
        [jnp.concatenate([part[:mid], part[mid:]], axis=1) for part in (high, low)], axis=0
    )
    both = jnp.dot(left, stacked, preferred_element_type=F32)
    both = both[:mid] + both[mid:]
    return jnp.concatenate([both[:, :LANES], both[:, LANES:]], axis=0)


def swap_halves(first, second):
    low = lax.broadcasted_iota(jnp.int32, first.shape, 1) < LANES // 2
    return (
        jnp.where(low, first, pltpu.roll(second, LANES // 2, 1)),
        jnp.where(low, pltpu.roll(first, LANES // 2, 1), second),
    )


def partner(parts, mask):
    return lax.axis_index("cols").astype(jnp.int32) ^ mask


def left_body(parts, x_ref, field_ref, right_ref, left_ref, *rest):
    outs, gain_ref, work = rest[:-2], rest[-2], rest[-1]
    rows = x_ref.shape[0]

    @pl.when(pl.program_id(0) == 0)
    def _():
        gain = [jnp.exp(coupling * (2.0 * field_ref[moment].astype(F32) - 1.0)) for moment in range(SLICES)]
        for moment in range(SLICES):
            for c in range(LX // 2):
                row = jnp.broadcast_to(gain[moment][:, c * LANES : (c + 1) * LANES], (8, LANES))
                even, odd = swap_halves(row, row)
                gain_ref[moment, 2 * c : 2 * c + 1, :] = even[:1]
                gain_ref[moment, 2 * c + 1 : 2 * c + 2, :] = odd[:1]

    for group in range(rows // 16):
        for c in range(LX // 2):
            lanes = slice(c * LANES, (c + 1) * LANES)
            even, odd = swap_halves(x_ref[group * 16 : group * 16 + 8, lanes], x_ref[group * 16 + 8 : group * 16 + 16, lanes])
            work[pl.ds(group * 8 * (LX + PAIR_PAD) + 2 * c, 8, stride=LX + PAIR_PAD), :] = even
            work[pl.ds(group * 8 * (LX + PAIR_PAD) + 2 * c + 1, 8, stride=LX + PAIR_PAD), :] = odd
    for moment in range(SLICES):
        gain = jnp.concatenate([gain_ref[moment]] * (TALL // LX), axis=0)
        pairs = TALL // LX
        for part in (lambda data: mix_lanes(data * gain, right_ref[...]), lambda data: mix_rows(left_ref[...], data)):
            for top in range(0, rows // 2, pairs):
                spans = [slice((top + q) * (LX + PAIR_PAD), (top + q) * (LX + PAIR_PAD) + LX) for q in range(pairs)]
                data = part(jnp.concatenate([work[span, :] for span in spans], axis=0))
                for q, span in enumerate(spans):
                    work[span, :] = data[q * LX : (q + 1) * LX]
    for mask in range(parts):
        for half in range(2):
            ref = outs[half * parts + mask]
            start = partner(parts, mask) * (LX // parts) + 2 * half
            for group in range(rows // 16):
                even = work[pl.ds(group * 8 * (LX + PAIR_PAD) + start, 8, stride=LX + PAIR_PAD), :]
                odd = work[pl.ds(group * 8 * (LX + PAIR_PAD) + start + 1, 8, stride=LX + PAIR_PAD), :]
                above, below = swap_halves(even, odd)
                ref[group * 16 : group * 16 + 8, :] = above
                ref[group * 16 + 8 : group * 16 + 16, :] = below


def left_chain(parts, block, x, field, right, left):
    rows, sites = x.shape
    whole = lambda array: pl.BlockSpec(array.shape, lambda g: (0,) * array.ndim)
    outs = pl.pallas_call(
        functools.partial(left_body, parts),
        grid=(rows // block,),
        in_specs=[pl.BlockSpec((block, sites), lambda g: (g, 0)), whole(field), whole(right), whole(left)],
        out_specs=[pl.BlockSpec((block, LANES), lambda g: (g, 0))] * (2 * parts),
        out_shape=[jax.ShapeDtypeStruct((rows, LANES), F32)] * (2 * parts),
        scratch_shapes=[pltpu.VMEM((SLICES, LX, LANES), F32), pltpu.VMEM((block // 2 * (LX + PAIR_PAD), LANES), F32)],
        compiler_params=pltpu.CompilerParams(vmem_limit_bytes=VMEM_LIMIT),
        cost_estimate=pl.CostEstimate(flops=rows * sites * 256 * 2 * 6, bytes_accessed=rows * sites * 8, transcendentals=0),
        name="left_chain",
    )(x, field, right, left)
    return outs[:parts], outs[parts:]


def right_body(parts, loss_ref, left_y_ref, left_x_ref, *rest):
    pieces, outs, work = rest[:parts], rest[parts:-1], rest[-1]
    sites = loss_ref.shape[0]
    local = sites // parts

    def rows_of(mask):
        return pl.ds(pl.multiple_of(partner(parts, mask) * local, local), local)

    rows = local // LY
    tall = LY + ROW_PAD

    def span(x):
        start = x * tall
        return pl.ds(pl.multiple_of(start, 8) if ROW_PAD % 8 == 0 else start, LY)

    for mask in range(parts):
        for row in range(rows):
            work[span(partner(parts, mask) * rows + row), :] = pieces[mask][row * LY : (row + 1) * LY, :]
    step = TALL // LX
    for moment in range(SLICES):

        @pl.loop(0, sites // TALL // UNROLL)
        def _(turn):
            for q in range(UNROLL):
                x = (turn * UNROLL + q) * step
                data = jnp.concatenate([work[span(x + r), :] for r in range(step)], axis=0)
                loss = loss_ref[pl.ds(pl.multiple_of(x * LY, TALL), TALL), moment : moment + 1]
                data = mix_rows(left_y_ref[...], data * loss)
                for r in range(step):
                    work[span(x + r), :] = data[r * LY : (r + 1) * LY]

        @pl.loop(0, LY // step // UNROLL)
        def _(turn):
            for r in range(UNROLL):
                y = (turn * UNROLL + r) * step
                data = jnp.concatenate([work[pl.ds(y + q, LX, stride=tall), :] for q in range(step)], axis=0)
                data = mix_rows(left_x_ref[...], data)
                for q in range(step):
                    work[pl.ds(y + q, LX, stride=tall), :] = data[q * LX : (q + 1) * LX]

    for mask in range(parts):
        for row in range(rows):
            outs[mask][row * LY : (row + 1) * LY, :] = work[span(partner(parts, mask) * rows + row), :]


def right_chain(parts, loss, left_y, left_x, pieces):
    sites = loss.shape[0]
    whole = lambda array: pl.BlockSpec(array.shape, lambda g: (0,) * array.ndim)
    return pl.pallas_call(
        functools.partial(right_body, parts),
        grid=(1,),
        in_specs=[whole(loss), whole(left_y), whole(left_x)] + [whole(piece) for piece in pieces],
        out_specs=[whole(piece) for piece in pieces],
        out_shape=[jax.ShapeDtypeStruct(piece.shape, F32) for piece in pieces],
        scratch_shapes=[pltpu.VMEM((sites // LY * (LY + ROW_PAD), LANES), F32)],
        compiler_params=pltpu.CompilerParams(vmem_limit_bytes=RIGHT_LIMIT),
        cost_estimate=pl.CostEstimate(flops=sites * LANES * 256 * 2 * 6, bytes_accessed=sites * LANES * 12, transcendentals=0),
        name="right_chain",
    )(loss, left_y, left_x, *pieces)


def place_body(parts, lane, held, *rest):
    blocks, out, landed, came, went = rest[:parts], rest[parts + held], rest[-3], rest[-2], rest[-1]
    local = out.shape[1] // parts
    copies = []
    for mask in range(parts):
        start = pl.multiple_of(partner(parts, mask) * local + lane, LANES)
        copies.append((
            pltpu.make_async_copy(blocks[mask], landed.at[mask], came.at[mask]),
            pltpu.make_async_copy(landed.at[mask], out.at[:, pl.ds(start, LANES)], went.at[mask]),
        ))
    for copy, _ in copies:
        copy.start()
    for copy, onward in copies:
        copy.wait()
        onward.start()
    for _, onward in copies:
        onward.wait()


def place(parts, lane, blocks, held=None):
    rows = blocks[0].shape[0]
    held = [] if held is None else [held]
    anywhere = pl.BlockSpec(memory_space=pl.ANY)
    return pl.pallas_call(
        functools.partial(place_body, parts, lane, len(held)),
        in_specs=[anywhere] * (parts + len(held)),
        out_specs=anywhere,
        out_shape=jax.ShapeDtypeStruct((rows, rows * parts), F32),
        scratch_shapes=[pltpu.VMEM((parts, rows, LANES), F32)] + [pltpu.SemaphoreType.DMA((parts,))] * 2,
        input_output_aliases={parts: 0} if held else {},
        compiler_params=pltpu.CompilerParams(vmem_limit_bytes=VMEM_LIMIT),
        cost_estimate=pl.CostEstimate(flops=0, bytes_accessed=rows * LANES * parts * 8, transcendentals=0),
        name="place",
    )(*blocks, *held)


def kernel(length, growth):
    indices = jnp.arange(length, dtype=jnp.int32)
    phases = indices[:, None] * indices[None, :] % length
    angles = 2.0 * jnp.pi * phases.astype(jnp.float32) / length
    cosines = jnp.cos(angles)
    sines = jnp.sin(angles)
    spectrum = jnp.exp(growth * jnp.cos(2.0 * jnp.pi * indices.astype(jnp.float32) / length))
    highest = lax.Precision.HIGHEST
    total = jnp.dot(cosines * spectrum[None, :], cosines.T, precision=highest)
    total = total + jnp.dot(sines * spectrum[None, :], sines.T, precision=highest)
    return total / length


def whole_exchange(green_by_column, field):
    highest = lax.Precision.HIGHEST
    walkers, local_cols, sites = green_by_column.shape
    fwd_x = kernel(LX, hop_rate)
    fwd_y = kernel(LY, hop_rate)
    inv_x = kernel(LX, -hop_rate)
    inv_y = kernel(LY, -hop_rate)
    spins = 2.0 * field.astype(jnp.float32) - 1.0
    green = green_by_column
    for moment in range(SLICES):
        left_green = green
        left_green = left_green * jnp.exp(coupling * spins[:, moment, :])[:, None, :]
        left_blocks = left_green.reshape(walkers, local_cols, LX, LY)
        left_blocks = jnp.einsum("xa,wcab->wcxb", fwd_x, left_blocks, precision=highest)
        left_blocks = jnp.einsum("yb,wcxb->wcxy", fwd_y, left_blocks, precision=highest)
        green = left_blocks.reshape(walkers, local_cols, sites)
    parts = lax.axis_size("cols")
    shaped_in = green.reshape(walkers, local_cols, parts, sites // parts)
    row_block = lax.all_to_all(shaped_in, "cols", split_axis=2, concat_axis=1, tiled=True)
    count = row_block.shape[0]
    width = row_block.shape[3]
    blocks = row_block.reshape(count, sites, width)
    for moment in range(SLICES):
        blocks = blocks * jnp.exp(-coupling * spins[:, moment, :])[:, :, None]
        shaped = blocks.reshape(count, LX, LY, width)
        shaped = jnp.einsum("by,wabr->wayr", inv_y, shaped, precision=highest)
        shaped = jnp.einsum("ax,wayr->wxyr", inv_x, shaped, precision=highest)
        blocks = shaped.reshape(count, sites, width)
    rows_done = blocks.reshape(count, sites, 1, width)
    rows_done = rows_done.reshape(walkers, sites, sites // parts)
    green = lax.all_to_all(rows_done, "cols", split_axis=1, concat_axis=2, tiled=True)
    return green


class Links:
    def __init__(self, parts):
        self.parts = parts
        self.sent = []
        self.after = None

    def send(self, block, mask):
        hold = [self.after] if self.after is not None else []
        back = len(self.sent) - IN_FLIGHT
        if back >= 0:
            hold.append(self.sent[back]["value"])
        if hold:
            got = lax.optimization_barrier(tuple([block] + hold))
            block = got[0]
            if back >= 0:
                self.sent[back]["value"] = got[-1]
        value = lax.ppermute(block, "cols", [(s, s ^ mask) for s in range(self.parts)])
        self.sent.append({"value": value})
        return self.sent[-1]


def send_order(parts, pattern):
    far = [m for pair in zip(range(3 * parts // 4, parts), range(parts // 2, 3 * parts // 4)) for m in pair]
    near = [m for pair in zip(range(parts // 4, parts // 2), range(1, parts // 4 + 1)) for m in pair][: parts // 2 - 1]
    order = []
    for kind in pattern:
        side = far if kind == "f" else near
        if side:
            order.append(side.pop(0))
    return order + near + far


def pipelined(green_by_column, field):
    _, rows, sites = green_by_column.shape
    parts = lax.axis_size("cols")
    x = green_by_column.reshape(rows, sites)
    loss = jnp.exp(-coupling * (2.0 * field[0].astype(F32) - 1.0)).T
    right = lane_side(circulant(LY, hop_rate))
    left = row_side(circulant(LX, hop_rate))
    left_y = row_side(circulant(LY, -hop_rate))
    left_x = row_side(circulant(LX, -hop_rate))
    links = Links(parts)

    def chain(pieces):
        return right_chain(parts, loss, left_y, left_x, [pieces[mask]["value"] for mask in range(parts)])

    halves_ = left_chain(parts, rows // 4, x, field.transpose(1, 0, 2), right, left)
    sent = [{0: {"value": blocks[0]}} for blocks in halves_]
    done = []
    for h in range(2):
        for at, mask in enumerate(send_order(parts, PATTERNS[h])):
            if h == 1 and at == LATE:
                done.append(chain(sent[0]))
                links.after = done[0][0]
            sent[h][mask] = links.send(halves_[h][mask], mask)
    back = []
    for h in range(2):
        back.append({0: {"value": done[h][0]}})
        for at, mask in enumerate(send_order(parts, PATTERNS[2 + h])):
            if h == 0 and at == AHEAD:
                done.append(chain(sent[1]))
                links.after = done[1][0]
            back[h][mask] = links.send(done[h][mask], mask)
    result = None
    for h in range(2):
        result = place(parts, h * LANES, [back[h][mask]["value"] for mask in range(parts)], result)
    return result.reshape(green_by_column.shape)


def shards(green_by_column, field):
    walkers, rows, sites = green_by_column.shape
    parts = lax.axis_size("cols")
    fits = walkers == 1 and rows == 256 and rows * parts == sites and parts & (parts - 1) == 0 and parts >= 8
    if fits and LX * LY == sites and LX == LY == 64:
        return pipelined(green_by_column, field)
    return whole_exchange(green_by_column, field)


def solution(mesh):
    return jax.shard_map(
        shards,
        mesh=mesh,
        in_specs=(P("walk", "cols", None), P("walk", None, None)),
        out_specs=P("walk", "cols", None),
        check_vma=False,
    )
```

```python
import functools
import jax
import jax.numpy as jnp
import ml_dtypes
import numpy as np
from jax import lax
from jax.experimental import pallas as pl
from jax.experimental.pallas import tpu as pltpu
from jax.sharding import PartitionSpec as P

LX = 64
LY = 64
SLICES = 3
hop_rate = 0.6
coupling = 0.65373
LANES = 128
TALL = 256
ROW_PAD = 8
PAIR_PAD = 8
UNROLL = 8
VMEM_LIMIT = 60 << 20
RIGHT_LIMIT = 24 << 20
IN_FLIGHT = 5
PATTERNS = ('ffnfnfnfnnfnnff', 'ffnfnfnfnfnfnfn', 'ffnfnfnfnfnfnfn', 'ffnfnfnfnnfnnff')
LATE = 5
AHEAD = 5
BF = jnp.bfloat16
F32 = jnp.float32


def circulant(length, growth):
    angles = 2.0 * np.pi * np.arange(length) / length
    column = np.cos(np.outer(np.arange(length), angles)) @ np.exp(growth * np.cos(angles)) / length
    differ = (np.arange(length)[:, None] - np.arange(length)[None, :]) % length
    return column[differ]


def split_matrix(matrix):
    high = matrix.astype(ml_dtypes.bfloat16)
    return high, (matrix - high.astype(np.float64)).astype(ml_dtypes.bfloat16)


def lane_side(matrix):
    high, low = split_matrix(np.kron(np.eye(LANES // matrix.shape[0]), matrix).T)
    return jnp.asarray(np.tile(np.concatenate([high, low], axis=1), (2, 1)))


def row_side(matrix):
    high, low = split_matrix(np.kron(np.eye(LANES // matrix.shape[0]), matrix))
    return jnp.asarray(np.tile(np.concatenate([high, low], axis=0), (1, 2)))


def halves(value):
    high = value.astype(BF)
    return high, (value - high.astype(F32)).astype(BF)


def mix_lanes(data, right):
    high, low = halves(data)
    both = jnp.dot(jnp.concatenate([high, low], axis=1), right, preferred_element_type=F32)
    return both[:, :LANES] + both[:, LANES:]


def mix_rows(left, data):
    high, low = halves(data)
    mid = data.shape[0] // 2
    stacked = jnp.concatenate(
        [jnp.concatenate([part[:mid], part[mid:]], axis=1) for part in (high, low)], axis=0
    )
    both = jnp.dot(left, stacked, preferred_element_type=F32)
    both = both[:mid] + both[mid:]
    return jnp.concatenate([both[:, :LANES], both[:, LANES:]], axis=0)


def swap_halves(first, second):
    low = lax.broadcasted_iota(jnp.int32, first.shape, 1) < LANES // 2
    return (
        jnp.where(low, first, pltpu.roll(second, LANES // 2, 1)),
        jnp.where(low, pltpu.roll(first, LANES // 2, 1), second),
    )


def partner(parts, mask):
    return lax.axis_index("cols").astype(jnp.int32) ^ mask


def left_body(parts, x_ref, field_ref, right_ref, left_ref, *rest):
    outs, gain_ref, work = rest[:-2], rest[-2], rest[-1]
    rows = x_ref.shape[0]

    @pl.when(pl.program_id(0) == 0)
    def _():
        gain = [jnp.exp(coupling * (2.0 * field_ref[moment].astype(F32) - 1.0)) for moment in range(SLICES)]
        for moment in range(SLICES):
            for c in range(LX // 2):
                row = jnp.broadcast_to(gain[moment][:, c * LANES : (c + 1) * LANES], (8, LANES))
                even, odd = swap_halves(row, row)
                gain_ref[moment, 2 * c : 2 * c + 1, :] = even[:1]
                gain_ref[moment, 2 * c + 1 : 2 * c + 2, :] = odd[:1]

    for group in range(rows // 16):
        for c in range(LX // 2):
            lanes = slice(c * LANES, (c + 1) * LANES)
            even, odd = swap_halves(x_ref[group * 16 : group * 16 + 8, lanes], x_ref[group * 16 + 8 : group * 16 + 16, lanes])
            work[pl.ds(group * 8 * (LX + PAIR_PAD) + 2 * c, 8, stride=LX + PAIR_PAD), :] = even
            work[pl.ds(group * 8 * (LX + PAIR_PAD) + 2 * c + 1, 8, stride=LX + PAIR_PAD), :] = odd
    for moment in range(SLICES):
        gain = jnp.concatenate([gain_ref[moment]] * (TALL // LX), axis=0)
        pairs = TALL // LX
        for part in (lambda data: mix_lanes(data * gain, right_ref[...]), lambda data: mix_rows(left_ref[...], data)):
            for top in range(0, rows // 2, pairs):
                spans = [slice((top + q) * (LX + PAIR_PAD), (top + q) * (LX + PAIR_PAD) + LX) for q in range(pairs)]
                data = part(jnp.concatenate([work[span, :] for span in spans], axis=0))
                for q, span in enumerate(spans):
                    work[span, :] = data[q * LX : (q + 1) * LX]
    for mask in range(parts):
        for half in range(2):
            ref = outs[half * parts + mask]
            start = partner(parts, mask) * (LX // parts) + 2 * half
            for group in range(rows // 16):
                even = work[pl.ds(group * 8 * (LX + PAIR_PAD) + start, 8, stride=LX + PAIR_PAD), :]
                odd = work[pl.ds(group * 8 * (LX + PAIR_PAD) + start + 1, 8, stride=LX + PAIR_PAD), :]
                above, below = swap_halves(even, odd)
                ref[group * 16 : group * 16 + 8, :] = above
                ref[group * 16 + 8 : group * 16 + 16, :] = below


def left_chain(parts, block, x, field, right, left):
    rows, sites = x.shape
    whole = lambda array: pl.BlockSpec(array.shape, lambda g: (0,) * array.ndim)
    outs = pl.pallas_call(
        functools.partial(left_body, parts),
        grid=(rows // block,),
        in_specs=[pl.BlockSpec((block, sites), lambda g: (g, 0)), whole(field), whole(right), whole(left)],
        out_specs=[pl.BlockSpec((block, LANES), lambda g: (g, 0))] * (2 * parts),
        out_shape=[jax.ShapeDtypeStruct((rows, LANES), F32)] * (2 * parts),
        scratch_shapes=[pltpu.VMEM((SLICES, LX, LANES), F32), pltpu.VMEM(((block // 2 + 1) * (LX + PAIR_PAD), LANES), F32)],
        compiler_params=pltpu.CompilerParams(vmem_limit_bytes=VMEM_LIMIT),
        cost_estimate=pl.CostEstimate(flops=rows * sites * 256 * 2 * 6, bytes_accessed=rows * sites * 8, transcendentals=0),
        name="left_chain",
    )(x, field, right, left)
    return outs[:parts], outs[parts:]


def right_body(parts, loss_ref, left_y_ref, left_x_ref, *rest):
    pieces, outs, work = rest[:parts], rest[parts:-1], rest[-1]
    sites = loss_ref.shape[0]
    local = sites // parts

    def rows_of(mask):
        return pl.ds(pl.multiple_of(partner(parts, mask) * local, local), local)

    rows = local // LY
    tall = LY + ROW_PAD

    def span(x):
        start = x * tall
        return pl.ds(pl.multiple_of(start, 8) if ROW_PAD % 8 == 0 else start, LY)

    for mask in range(parts):
        for row in range(rows):
            work[span(partner(parts, mask) * rows + row), :] = pieces[mask][row * LY : (row + 1) * LY, :]
    step = TALL // LX
    for moment in range(SLICES):

        @pl.loop(0, sites // TALL // UNROLL)
        def _(turn):
            for q in range(UNROLL):
                x = (turn * UNROLL + q) * step
                data = jnp.concatenate([work[span(x + r), :] for r in range(step)], axis=0)
                loss = loss_ref[pl.ds(pl.multiple_of(x * LY, TALL), TALL), moment : moment + 1]
                data = mix_rows(left_y_ref[...], data * loss)
                for r in range(step):
                    work[span(x + r), :] = data[r * LY : (r + 1) * LY]

        @pl.loop(0, LY // step // UNROLL)
        def _(turn):
            for r in range(UNROLL):
                y = (turn * UNROLL + r) * step
                data = jnp.concatenate([work[pl.ds(y + q, LX, stride=tall), :] for q in range(step)], axis=0)
                data = mix_rows(left_x_ref[...], data)
                for q in range(step):
                    work[pl.ds(y + q, LX, stride=tall), :] = data[q * LX : (q + 1) * LX]

    for mask in range(parts):
        for row in range(rows):
            outs[mask][row * LY : (row + 1) * LY, :] = work[span(partner(parts, mask) * rows + row), :]


def right_chain(parts, loss, left_y, left_x, pieces):
    sites = loss.shape[0]
    whole = lambda array: pl.BlockSpec(array.shape, lambda g: (0,) * array.ndim)
    return pl.pallas_call(
        functools.partial(right_body, parts),
        grid=(1,),
        in_specs=[whole(loss), whole(left_y), whole(left_x)] + [whole(piece) for piece in pieces],
        out_specs=[whole(piece) for piece in pieces],
        out_shape=[jax.ShapeDtypeStruct(piece.shape, F32) for piece in pieces],
        scratch_shapes=[pltpu.VMEM(((sites // LY + 1) * (LY + ROW_PAD), LANES), F32)],
        compiler_params=pltpu.CompilerParams(vmem_limit_bytes=RIGHT_LIMIT),
        cost_estimate=pl.CostEstimate(flops=sites * LANES * 256 * 2 * 6, bytes_accessed=sites * LANES * 12, transcendentals=0),
        name="right_chain",
    )(loss, left_y, left_x, *pieces)


def place_body(parts, lane, held, *rest):
    blocks, out, landed, came, went = rest[:parts], rest[parts + held], rest[-3], rest[-2], rest[-1]
    local = out.shape[1] // parts
    copies = []
    for mask in range(parts):
        start = pl.multiple_of(partner(parts, mask) * local + lane, LANES)
        copies.append((
            pltpu.make_async_copy(blocks[mask], landed.at[mask], came.at[mask]),
            pltpu.make_async_copy(landed.at[mask], out.at[:, pl.ds(start, LANES)], went.at[mask]),
        ))
    for copy, _ in copies:
        copy.start()
    for copy, onward in copies:
        copy.wait()
        onward.start()
    for _, onward in copies:
        onward.wait()


def place(parts, lane, blocks, held=None):
    rows = blocks[0].shape[0]
    held = [] if held is None else [held]
    anywhere = pl.BlockSpec(memory_space=pl.ANY)
    return pl.pallas_call(
        functools.partial(place_body, parts, lane, len(held)),
        in_specs=[anywhere] * (parts + len(held)),
        out_specs=anywhere,
        out_shape=jax.ShapeDtypeStruct((rows, rows * parts), F32),
        scratch_shapes=[pltpu.VMEM((parts, rows, LANES), F32)] + [pltpu.SemaphoreType.DMA((parts,))] * 2,
        input_output_aliases={parts: 0} if held else {},
        compiler_params=pltpu.CompilerParams(vmem_limit_bytes=VMEM_LIMIT),
        cost_estimate=pl.CostEstimate(flops=0, bytes_accessed=rows * LANES * parts * 8, transcendentals=0),
        name="place",
    )(*blocks, *held)


def kernel(length, growth):
    indices = jnp.arange(length, dtype=jnp.int32)
    phases = indices[:, None] * indices[None, :] % length
    angles = 2.0 * jnp.pi * phases.astype(jnp.float32) / length
    cosines = jnp.cos(angles)
    sines = jnp.sin(angles)
    spectrum = jnp.exp(growth * jnp.cos(2.0 * jnp.pi * indices.astype(jnp.float32) / length))
    highest = lax.Precision.HIGHEST
    total = jnp.dot(cosines * spectrum[None, :], cosines.T, precision=highest)
    total = total + jnp.dot(sines * spectrum[None, :], sines.T, precision=highest)
    return total / length


def whole_exchange(green_by_column, field):
    highest = lax.Precision.HIGHEST
    walkers, local_cols, sites = green_by_column.shape
    fwd_x = kernel(LX, hop_rate)
    fwd_y = kernel(LY, hop_rate)
    inv_x = kernel(LX, -hop_rate)
    inv_y = kernel(LY, -hop_rate)
    spins = 2.0 * field.astype(jnp.float32) - 1.0
    green = green_by_column
    for moment in range(SLICES):
        left_green = green
        left_green = left_green * jnp.exp(coupling * spins[:, moment, :])[:, None, :]
        left_blocks = left_green.reshape(walkers, local_cols, LX, LY)
        left_blocks = jnp.einsum("xa,wcab->wcxb", fwd_x, left_blocks, precision=highest)
        left_blocks = jnp.einsum("yb,wcxb->wcxy", fwd_y, left_blocks, precision=highest)
        green = left_blocks.reshape(walkers, local_cols, sites)
    parts = lax.axis_size("cols")
    shaped_in = green.reshape(walkers, local_cols, parts, sites // parts)
    row_block = lax.all_to_all(shaped_in, "cols", split_axis=2, concat_axis=1, tiled=True)
    count = row_block.shape[0]
    width = row_block.shape[3]
    blocks = row_block.reshape(count, sites, width)
    for moment in range(SLICES):
        blocks = blocks * jnp.exp(-coupling * spins[:, moment, :])[:, :, None]
        shaped = blocks.reshape(count, LX, LY, width)
        shaped = jnp.einsum("by,wabr->wayr", inv_y, shaped, precision=highest)
        shaped = jnp.einsum("ax,wayr->wxyr", inv_x, shaped, precision=highest)
        blocks = shaped.reshape(count, sites, width)
    rows_done = blocks.reshape(count, sites, 1, width)
    rows_done = rows_done.reshape(walkers, sites, sites // parts)
    green = lax.all_to_all(rows_done, "cols", split_axis=1, concat_axis=2, tiled=True)
    return green


class Links:
    def __init__(self, parts):
        self.parts = parts
        self.sent = []
        self.after = None

    def send(self, block, mask):
        hold = [self.after] if self.after is not None else []
        back = len(self.sent) - IN_FLIGHT
        if back >= 0:
            hold.append(self.sent[back]["value"])
        if hold:
            got = lax.optimization_barrier(tuple([block] + hold))
            block = got[0]
            if back >= 0:
                self.sent[back]["value"] = got[-1]
        value = lax.ppermute(block, "cols", [(s, s ^ mask) for s in range(self.parts)])
        self.sent.append({"value": value})
        return self.sent[-1]


def send_order(parts, pattern):
    far = [m for pair in zip(range(3 * parts // 4, parts), range(parts // 2, 3 * parts // 4)) for m in pair]
    near = [m for pair in zip(range(parts // 4, parts // 2), range(1, parts // 4 + 1)) for m in pair][: parts // 2 - 1]
    order = []
    for kind in pattern:
        side = far if kind == "f" else near
        if side:
            order.append(side.pop(0))
    return order + near + far


def pipelined(green_by_column, field):
    _, rows, sites = green_by_column.shape
    parts = lax.axis_size("cols")
    x = green_by_column.reshape(rows, sites)
    loss = jnp.exp(-coupling * (2.0 * field[0].astype(F32) - 1.0)).T
    right = lane_side(circulant(LY, hop_rate))
    left = row_side(circulant(LX, hop_rate))
    left_y = row_side(circulant(LY, -hop_rate))
    left_x = row_side(circulant(LX, -hop_rate))
    links = Links(parts)

    def chain(pieces):
        return right_chain(parts, loss, left_y, left_x, [pieces[mask]["value"] for mask in range(parts)])

    halves_ = left_chain(parts, rows // 4, x, field.transpose(1, 0, 2), right, left)
    sent = [{0: {"value": blocks[0]}} for blocks in halves_]
    done = []
    for h in range(2):
        for at, mask in enumerate(send_order(parts, PATTERNS[h])):
            if h == 1 and at == LATE:
                done.append(chain(sent[0]))
                links.after = done[0][0]
            sent[h][mask] = links.send(halves_[h][mask], mask)
    back = []
    for h in range(2):
        back.append({0: {"value": done[h][0]}})
        for at, mask in enumerate(send_order(parts, PATTERNS[2 + h])):
            if h == 0 and at == AHEAD:
                done.append(chain(sent[1]))
                links.after = done[1][0]
            back[h][mask] = links.send(done[h][mask], mask)
    result = None
    for h in range(2):
        result = place(parts, h * LANES, [back[h][mask]["value"] for mask in range(parts)], result)
    return result.reshape(green_by_column.shape)


def shards(green_by_column, field):
    walkers, rows, sites = green_by_column.shape
    parts = lax.axis_size("cols")
    fits = walkers == 1 and rows == 256 and rows * parts == sites and parts & (parts - 1) == 0 and parts >= 8
    if fits and LX * LY == sites and LX == LY == 64:
        return pipelined(green_by_column, field)
    return whole_exchange(green_by_column, field)


def solution(mesh):
    return jax.shard_map(
        shards,
        mesh=mesh,
        in_specs=(P("walk", "cols", None), P("walk", None, None)),
        out_specs=P("walk", "cols", None),
        check_vma=False,
    )
```

```python
import functools
import jax
import jax.numpy as jnp
import ml_dtypes
import numpy as np
from jax import lax
from jax.experimental import pallas as pl
from jax.experimental.pallas import tpu as pltpu
from jax.sharding import PartitionSpec as P

LX = 64
LY = 64
SLICES = 3
hop_rate = 0.6
coupling = 0.65373
LANES = 128
TALL = 256
ROW_PAD = 8
PAIR_PAD = 8
UNROLL = 8
VMEM_LIMIT = 60 << 20
PLACE_LIMIT = 16 << 20
RIGHT_LIMIT = 24 << 20
IN_FLIGHT = 5
PATTERNS = ('ffnfnfnfnnfnnff', 'ffnfnfnfnfnfnfn', 'ffnfnfnfnfnfnfn', 'ffnfnfnfnnfnnff')
LATE = 5
AHEAD = 5
BF = jnp.bfloat16
F32 = jnp.float32


def circulant(length, growth):
    angles = 2.0 * np.pi * np.arange(length) / length
    column = np.cos(np.outer(np.arange(length), angles)) @ np.exp(growth * np.cos(angles)) / length
    differ = (np.arange(length)[:, None] - np.arange(length)[None, :]) % length
    return column[differ]


def split_matrix(matrix):
    high = matrix.astype(ml_dtypes.bfloat16)
    return high, (matrix - high.astype(np.float64)).astype(ml_dtypes.bfloat16)


def lane_side(matrix):
    high, low = split_matrix(np.kron(np.eye(LANES // matrix.shape[0]), matrix).T)
    return jnp.asarray(np.tile(np.concatenate([high, low], axis=1), (2, 1)))


def row_side(matrix):
    high, low = split_matrix(np.kron(np.eye(LANES // matrix.shape[0]), matrix))
    return jnp.asarray(np.tile(np.concatenate([high, low], axis=0), (1, 2)))


def halves(value):
    high = value.astype(BF)
    return high, (value - high.astype(F32)).astype(BF)


def mix_lanes(data, right):
    high, low = halves(data)
    both = jnp.dot(jnp.concatenate([high, low], axis=1), right, preferred_element_type=F32)
    return both[:, :LANES] + both[:, LANES:]


def mix_rows(left, data):
    high, low = halves(data)
    mid = data.shape[0] // 2
    stacked = jnp.concatenate(
        [jnp.concatenate([part[:mid], part[mid:]], axis=1) for part in (high, low)], axis=0
    )
    both = jnp.dot(left, stacked, preferred_element_type=F32)
    both = both[:mid] + both[mid:]
    return jnp.concatenate([both[:, :LANES], both[:, LANES:]], axis=0)


def swap_halves(first, second):
    low = lax.broadcasted_iota(jnp.int32, first.shape, 1) < LANES // 2
    return (
        jnp.where(low, first, pltpu.roll(second, LANES // 2, 1)),
        jnp.where(low, pltpu.roll(first, LANES // 2, 1), second),
    )


def partner(parts, mask):
    return lax.axis_index("cols").astype(jnp.int32) ^ mask


def left_body(parts, x_ref, field_ref, right_ref, left_ref, *rest):
    outs, gain_ref, work = rest[:-2], rest[-2], rest[-1]
    rows = x_ref.shape[0]

    @pl.when(pl.program_id(0) == 0)
    def _():
        gain = [jnp.exp(coupling * (2.0 * field_ref[moment].astype(F32) - 1.0)) for moment in range(SLICES)]
        for moment in range(SLICES):
            for c in range(LX // 2):
                row = jnp.broadcast_to(gain[moment][:, c * LANES : (c + 1) * LANES], (8, LANES))
                even, odd = swap_halves(row, row)
                gain_ref[moment, 2 * c : 2 * c + 1, :] = even[:1]
                gain_ref[moment, 2 * c + 1 : 2 * c + 2, :] = odd[:1]

    for group in range(rows // 16):
        for c in range(LX // 2):
            lanes = slice(c * LANES, (c + 1) * LANES)
            even, odd = swap_halves(x_ref[group * 16 : group * 16 + 8, lanes], x_ref[group * 16 + 8 : group * 16 + 16, lanes])
            work[pl.ds(group * 8 * (LX + PAIR_PAD) + 2 * c, 8, stride=LX + PAIR_PAD), :] = even
            work[pl.ds(group * 8 * (LX + PAIR_PAD) + 2 * c + 1, 8, stride=LX + PAIR_PAD), :] = odd
    for moment in range(SLICES):
        gain = jnp.concatenate([gain_ref[moment]] * (TALL // LX), axis=0)
        pairs = TALL // LX
        for part in (lambda data: mix_lanes(data * gain, right_ref[...]), lambda data: mix_rows(left_ref[...], data)):
            for top in range(0, rows // 2, pairs):
                spans = [slice((top + q) * (LX + PAIR_PAD), (top + q) * (LX + PAIR_PAD) + LX) for q in range(pairs)]
                data = part(jnp.concatenate([work[span, :] for span in spans], axis=0))
                for q, span in enumerate(spans):
                    work[span, :] = data[q * LX : (q + 1) * LX]
    for mask in range(parts):
        for half in range(2):
            ref = outs[half * parts + mask]
            start = partner(parts, mask) * (LX // parts) + 2 * half
            for group in range(rows // 16):
                even = work[pl.ds(group * 8 * (LX + PAIR_PAD) + start, 8, stride=LX + PAIR_PAD), :]
                odd = work[pl.ds(group * 8 * (LX + PAIR_PAD) + start + 1, 8, stride=LX + PAIR_PAD), :]
                above, below = swap_halves(even, odd)
                ref[group * 16 : group * 16 + 8, :] = above
                ref[group * 16 + 8 : group * 16 + 16, :] = below


def left_chain(parts, block, x, field, right, left):
    rows, sites = x.shape
    whole = lambda array: pl.BlockSpec(array.shape, lambda g: (0,) * array.ndim)
    outs = pl.pallas_call(
        functools.partial(left_body, parts),
        grid=(rows // block,),
        in_specs=[pl.BlockSpec((block, sites), lambda g: (g, 0)), whole(field), whole(right), whole(left)],
        out_specs=[pl.BlockSpec((block, LANES), lambda g: (g, 0))] * (2 * parts),
        out_shape=[jax.ShapeDtypeStruct((rows, LANES), F32)] * (2 * parts),
        scratch_shapes=[pltpu.VMEM((SLICES, LX, LANES), F32), pltpu.VMEM(((block // 2 + 1) * (LX + PAIR_PAD), LANES), F32)],
        compiler_params=pltpu.CompilerParams(vmem_limit_bytes=VMEM_LIMIT),
        cost_estimate=pl.CostEstimate(flops=rows * sites * 256 * 2 * 6, bytes_accessed=rows * sites * 8, transcendentals=0),
        name="left_chain",
    )(x, field, right, left)
    return outs[:parts], outs[parts:]


def right_body(parts, loss_ref, left_y_ref, left_x_ref, *rest):
    pieces, outs, work = rest[:parts], rest[parts:-1], rest[-1]
    sites = loss_ref.shape[0]
    local = sites // parts

    def rows_of(mask):
        return pl.ds(pl.multiple_of(partner(parts, mask) * local, local), local)

    rows = local // LY
    tall = LY + ROW_PAD

    def span(x):
        start = x * tall
        return pl.ds(pl.multiple_of(start, 8) if ROW_PAD % 8 == 0 else start, LY)

    for mask in range(parts):
        for row in range(rows):
            work[span(partner(parts, mask) * rows + row), :] = pieces[mask][row * LY : (row + 1) * LY, :]
    step = TALL // LX
    for moment in range(SLICES):

        @pl.loop(0, sites // TALL // UNROLL)
        def _(turn):
            for q in range(UNROLL):
                x = (turn * UNROLL + q) * step
                data = jnp.concatenate([work[span(x + r), :] for r in range(step)], axis=0)
                loss = loss_ref[pl.ds(pl.multiple_of(x * LY, TALL), TALL), moment : moment + 1]
                data = mix_rows(left_y_ref[...], data * loss)
                for r in range(step):
                    work[span(x + r), :] = data[r * LY : (r + 1) * LY]

        @pl.loop(0, LY // step // UNROLL)
        def _(turn):
            for r in range(UNROLL):
                y = (turn * UNROLL + r) * step
                data = jnp.concatenate([work[pl.ds(y + q, LX, stride=tall), :] for q in range(step)], axis=0)
                data = mix_rows(left_x_ref[...], data)
                for q in range(step):
                    work[pl.ds(y + q, LX, stride=tall), :] = data[q * LX : (q + 1) * LX]

    for mask in range(parts):
        for row in range(rows):
            outs[mask][row * LY : (row + 1) * LY, :] = work[span(partner(parts, mask) * rows + row), :]


def right_chain(parts, loss, left_y, left_x, pieces):
    sites = loss.shape[0]
    whole = lambda array: pl.BlockSpec(array.shape, lambda g: (0,) * array.ndim)
    return pl.pallas_call(
        functools.partial(right_body, parts),
        grid=(1,),
        in_specs=[whole(loss), whole(left_y), whole(left_x)] + [whole(piece) for piece in pieces],
        out_specs=[whole(piece) for piece in pieces],
        out_shape=[jax.ShapeDtypeStruct(piece.shape, F32) for piece in pieces],
        scratch_shapes=[pltpu.VMEM(((sites // LY + 1) * (LY + ROW_PAD), LANES), F32)],
        compiler_params=pltpu.CompilerParams(vmem_limit_bytes=RIGHT_LIMIT),
        cost_estimate=pl.CostEstimate(flops=sites * LANES * 256 * 2 * 6, bytes_accessed=sites * LANES * 12, transcendentals=0),
        name="right_chain",
    )(loss, left_y, left_x, *pieces)


def place_body(parts, lane, held, *rest):
    blocks, out, sems = rest[:parts], rest[parts + held], rest[-1]
    local = out.shape[1] // parts
    copies = []
    for mask in range(parts):
        start = pl.multiple_of(partner(parts, mask) * local + lane, LANES)
        copies.append(pltpu.make_async_copy(blocks[mask], out.at[:, pl.ds(start, LANES)], sems.at[mask]))
    for copy in copies:
        copy.start()
    for copy in copies:
        copy.wait()


def place(parts, lane, blocks, held=None):
    rows = blocks[0].shape[0]
    held = [] if held is None else [held]
    anywhere = pl.BlockSpec(memory_space=pl.ANY)
    return pl.pallas_call(
        functools.partial(place_body, parts, lane, len(held)),
        in_specs=[pl.BlockSpec(memory_space=pltpu.VMEM)] * parts + [anywhere] * len(held),
        out_specs=anywhere,
        out_shape=jax.ShapeDtypeStruct((rows, rows * parts), F32),
        scratch_shapes=[pltpu.SemaphoreType.DMA((parts,))],
        input_output_aliases={parts: 0} if held else {},
        compiler_params=pltpu.CompilerParams(vmem_limit_bytes=PLACE_LIMIT),
        cost_estimate=pl.CostEstimate(flops=0, bytes_accessed=rows * LANES * parts * 8, transcendentals=0),
        name="place",
    )(*blocks, *held)


def kernel(length, growth):
    indices = jnp.arange(length, dtype=jnp.int32)
    phases = indices[:, None] * indices[None, :] % length
    angles = 2.0 * jnp.pi * phases.astype(jnp.float32) / length
    cosines = jnp.cos(angles)
    sines = jnp.sin(angles)
    spectrum = jnp.exp(growth * jnp.cos(2.0 * jnp.pi * indices.astype(jnp.float32) / length))
    highest = lax.Precision.HIGHEST
    total = jnp.dot(cosines * spectrum[None, :], cosines.T, precision=highest)
    total = total + jnp.dot(sines * spectrum[None, :], sines.T, precision=highest)
    return total / length


def whole_exchange(green_by_column, field):
    highest = lax.Precision.HIGHEST
    walkers, local_cols, sites = green_by_column.shape
    fwd_x = kernel(LX, hop_rate)
    fwd_y = kernel(LY, hop_rate)
    inv_x = kernel(LX, -hop_rate)
    inv_y = kernel(LY, -hop_rate)
    spins = 2.0 * field.astype(jnp.float32) - 1.0
    green = green_by_column
    for moment in range(SLICES):
        left_green = green
        left_green = left_green * jnp.exp(coupling * spins[:, moment, :])[:, None, :]
        left_blocks = left_green.reshape(walkers, local_cols, LX, LY)
        left_blocks = jnp.einsum("xa,wcab->wcxb", fwd_x, left_blocks, precision=highest)
        left_blocks = jnp.einsum("yb,wcxb->wcxy", fwd_y, left_blocks, precision=highest)
        green = left_blocks.reshape(walkers, local_cols, sites)
    parts = lax.axis_size("cols")
    shaped_in = green.reshape(walkers, local_cols, parts, sites // parts)
    row_block = lax.all_to_all(shaped_in, "cols", split_axis=2, concat_axis=1, tiled=True)
    count = row_block.shape[0]
    width = row_block.shape[3]
    blocks = row_block.reshape(count, sites, width)
    for moment in range(SLICES):
        blocks = blocks * jnp.exp(-coupling * spins[:, moment, :])[:, :, None]
        shaped = blocks.reshape(count, LX, LY, width)
        shaped = jnp.einsum("by,wabr->wayr", inv_y, shaped, precision=highest)
        shaped = jnp.einsum("ax,wayr->wxyr", inv_x, shaped, precision=highest)
        blocks = shaped.reshape(count, sites, width)
    rows_done = blocks.reshape(count, sites, 1, width)
    rows_done = rows_done.reshape(walkers, sites, sites // parts)
    green = lax.all_to_all(rows_done, "cols", split_axis=1, concat_axis=2, tiled=True)
    return green


class Links:
    def __init__(self, parts):
        self.parts = parts
        self.sent = []
        self.after = None

    def send(self, block, mask):
        hold = [self.after] if self.after is not None else []
        back = len(self.sent) - IN_FLIGHT
        if back >= 0:
            hold.append(self.sent[back]["value"])
        if hold:
            got = lax.optimization_barrier(tuple([block] + hold))
            block = got[0]
            if back >= 0:
                self.sent[back]["value"] = got[-1]
        value = lax.ppermute(block, "cols", [(s, s ^ mask) for s in range(self.parts)])
        self.sent.append({"value": value})
        return self.sent[-1]


def send_order(parts, pattern):
    far = [m for pair in zip(range(3 * parts // 4, parts), range(parts // 2, 3 * parts // 4)) for m in pair]
    near = [m for pair in zip(range(parts // 4, parts // 2), range(1, parts // 4 + 1)) for m in pair][: parts // 2 - 1]
    order = []
    for kind in pattern:
        side = far if kind == "f" else near
        if side:
            order.append(side.pop(0))
    return order + near + far


def pipelined(green_by_column, field):
    _, rows, sites = green_by_column.shape
    parts = lax.axis_size("cols")
    x = green_by_column.reshape(rows, sites)
    loss = jnp.exp(-coupling * (2.0 * field[0].astype(F32) - 1.0)).T
    right = lane_side(circulant(LY, hop_rate))
    left = row_side(circulant(LX, hop_rate))
    left_y = row_side(circulant(LY, -hop_rate))
    left_x = row_side(circulant(LX, -hop_rate))
    links = Links(parts)

    def chain(pieces):
        return right_chain(parts, loss, left_y, left_x, [pieces[mask]["value"] for mask in range(parts)])

    halves_ = left_chain(parts, rows // 4, x, field.transpose(1, 0, 2), right, left)
    sent = [{0: {"value": blocks[0]}} for blocks in halves_]
    done = []
    for h in range(2):
        for at, mask in enumerate(send_order(parts, PATTERNS[h])):
            if h == 1 and at == LATE:
                done.append(chain(sent[0]))
                links.after = done[0][0]
            sent[h][mask] = links.send(halves_[h][mask], mask)
    back = []
    for h in range(2):
        back.append({0: {"value": done[h][0]}})
        for at, mask in enumerate(send_order(parts, PATTERNS[2 + h])):
            if h == 0 and at == AHEAD:
                done.append(chain(sent[1]))
                links.after = done[1][0]
            back[h][mask] = links.send(done[h][mask], mask)
    result = None
    for h in range(2):
        result = place(parts, h * LANES, [back[h][mask]["value"] for mask in range(parts)], result)
    return result.reshape(green_by_column.shape)


def shards(green_by_column, field):
    walkers, rows, sites = green_by_column.shape
    parts = lax.axis_size("cols")
    fits = walkers == 1 and rows == 256 and rows * parts == sites and parts & (parts - 1) == 0 and parts >= 8
    if fits and LX * LY == sites and LX == LY == 64:
        return pipelined(green_by_column, field)
    return whole_exchange(green_by_column, field)


def solution(mesh):
    return jax.shard_map(
        shards,
        mesh=mesh,
        in_specs=(P("walk", "cols", None), P("walk", None, None)),
        out_specs=P("walk", "cols", None),
        check_vma=False,
    )
```

```python
import functools
import jax
import jax.numpy as jnp
import ml_dtypes
import numpy as np
from jax import lax
from jax.experimental import pallas as pl
from jax.experimental.pallas import tpu as pltpu
from jax.sharding import PartitionSpec as P

LX = 64
LY = 64
SLICES = 3
hop_rate = 0.6
coupling = 0.65373
LANES = 128
TALL = 256
ROW_PAD = 8
PAIR_PAD = 8
UNROLL = 8
VMEM_LIMIT = 60 << 20
PLACE_LIMIT = 16 << 20
RIGHT_LIMIT = 24 << 20
IN_FLIGHT = 5
PATTERNS = ('ffnfnfnfnnfnnff', 'ffnfnfnfnfnfnfn', 'ffnfnfnfnfnfnfn', 'nfnfnfnfnfnfnff')
LATE = 5
AHEAD = 5
BF = jnp.bfloat16
F32 = jnp.float32


def circulant(length, growth):
    angles = 2.0 * np.pi * np.arange(length) / length
    column = np.cos(np.outer(np.arange(length), angles)) @ np.exp(growth * np.cos(angles)) / length
    differ = (np.arange(length)[:, None] - np.arange(length)[None, :]) % length
    return column[differ]


def split_matrix(matrix):
    high = matrix.astype(ml_dtypes.bfloat16)
    return high, (matrix - high.astype(np.float64)).astype(ml_dtypes.bfloat16)


def steady(matrix):
    column = matrix[:, 0]
    spectrum = np.fft.fft(column).real

    def fault(factor):
        high, low = split_matrix(factor * column)
        kept = (high.astype(np.float64) + low.astype(np.float64)) / factor
        return np.abs(np.fft.fft(kept - column).real / spectrum).max()

    factor = min((1.0 + step / 1000.0 for step in range(1000)), key=fault)
    return factor * matrix, factor


def lane_side(matrix):
    high, low = split_matrix(np.kron(np.eye(LANES // matrix.shape[0]), matrix).T)
    return jnp.asarray(np.tile(np.concatenate([high, low], axis=1), (2, 1)))


def row_side(matrix):
    high, low = split_matrix(np.kron(np.eye(LANES // matrix.shape[0]), matrix))
    return jnp.asarray(np.tile(np.concatenate([high, low], axis=0), (1, 2)))


def halves(value):
    high = value.astype(BF)
    return high, (value - high.astype(F32)).astype(BF)


def mix_lanes(data, right):
    high, low = halves(data)
    both = jnp.dot(jnp.concatenate([high, low], axis=1), right, preferred_element_type=F32)
    return both[:, :LANES] + both[:, LANES:]


def mix_rows(left, data):
    high, low = halves(data)
    mid = data.shape[0] // 2
    stacked = jnp.concatenate(
        [jnp.concatenate([part[:mid], part[mid:]], axis=1) for part in (high, low)], axis=0
    )
    both = jnp.dot(left, stacked, preferred_element_type=F32)
    both = both[:mid] + both[mid:]
    return jnp.concatenate([both[:, :LANES], both[:, LANES:]], axis=0)


def swap_halves(first, second):
    low = lax.broadcasted_iota(jnp.int32, first.shape, 1) < LANES // 2
    return (
        jnp.where(low, first, pltpu.roll(second, LANES // 2, 1)),
        jnp.where(low, pltpu.roll(first, LANES // 2, 1), second),
    )


def partner(parts, mask):
    return lax.axis_index("cols").astype(jnp.int32) ^ mask


def left_body(parts, shrink, x_ref, field_ref, right_ref, left_ref, *rest):
    outs, gain_ref, work = rest[:-2], rest[-2], rest[-1]
    rows = x_ref.shape[0]

    @pl.when(pl.program_id(0) == 0)
    def _():
        gain = [shrink * jnp.exp(coupling * (2.0 * field_ref[moment].astype(F32) - 1.0)) for moment in range(SLICES)]
        for moment in range(SLICES):
            for c in range(LX // 2):
                row = jnp.broadcast_to(gain[moment][:, c * LANES : (c + 1) * LANES], (8, LANES))
                even, odd = swap_halves(row, row)
                gain_ref[moment, 2 * c : 2 * c + 1, :] = even[:1]
                gain_ref[moment, 2 * c + 1 : 2 * c + 2, :] = odd[:1]

    for group in range(rows // 16):
        for c in range(LX // 2):
            lanes = slice(c * LANES, (c + 1) * LANES)
            even, odd = swap_halves(x_ref[group * 16 : group * 16 + 8, lanes], x_ref[group * 16 + 8 : group * 16 + 16, lanes])
            work[pl.ds(group * 8 * (LX + PAIR_PAD) + 2 * c, 8, stride=LX + PAIR_PAD), :] = even
            work[pl.ds(group * 8 * (LX + PAIR_PAD) + 2 * c + 1, 8, stride=LX + PAIR_PAD), :] = odd
    for moment in range(SLICES):
        gain = jnp.concatenate([gain_ref[moment]] * (TALL // LX), axis=0)
        pairs = TALL // LX
        for part in (lambda data: mix_lanes(data * gain, right_ref[...]), lambda data: mix_rows(left_ref[...], data)):
            for top in range(0, rows // 2, pairs):
                spans = [slice((top + q) * (LX + PAIR_PAD), (top + q) * (LX + PAIR_PAD) + LX) for q in range(pairs)]
                data = part(jnp.concatenate([work[span, :] for span in spans], axis=0))
                for q, span in enumerate(spans):
                    work[span, :] = data[q * LX : (q + 1) * LX]
    for mask in range(parts):
        for half in range(2):
            ref = outs[half * parts + mask]
            start = partner(parts, mask) * (LX // parts) + 2 * half
            for group in range(rows // 16):
                even = work[pl.ds(group * 8 * (LX + PAIR_PAD) + start, 8, stride=LX + PAIR_PAD), :]
                odd = work[pl.ds(group * 8 * (LX + PAIR_PAD) + start + 1, 8, stride=LX + PAIR_PAD), :]
                above, below = swap_halves(even, odd)
                ref[group * 16 : group * 16 + 8, :] = above
                ref[group * 16 + 8 : group * 16 + 16, :] = below


def left_chain(parts, shrink, block, x, field, right, left):
    rows, sites = x.shape
    whole = lambda array: pl.BlockSpec(array.shape, lambda g: (0,) * array.ndim)
    outs = pl.pallas_call(
        functools.partial(left_body, parts, shrink),
        grid=(rows // block,),
        in_specs=[pl.BlockSpec((block, sites), lambda g: (g, 0)), whole(field), whole(right), whole(left)],
        out_specs=[pl.BlockSpec((block, LANES), lambda g: (g, 0))] * (2 * parts),
        out_shape=[jax.ShapeDtypeStruct((rows, LANES), F32)] * (2 * parts),
        scratch_shapes=[pltpu.VMEM((SLICES, LX, LANES), F32), pltpu.VMEM(((block // 2 + 1) * (LX + PAIR_PAD), LANES), F32)],
        compiler_params=pltpu.CompilerParams(vmem_limit_bytes=VMEM_LIMIT),
        cost_estimate=pl.CostEstimate(flops=rows * sites * 256 * 2 * 6, bytes_accessed=rows * sites * 8, transcendentals=0),
        name="left_chain",
    )(x, field, right, left)
    return outs[:parts], outs[parts:]


def right_body(parts, loss_ref, left_y_ref, left_x_ref, *rest):
    pieces, outs, work = rest[:parts], rest[parts:-1], rest[-1]
    sites = loss_ref.shape[0]
    local = sites // parts

    def rows_of(mask):
        return pl.ds(pl.multiple_of(partner(parts, mask) * local, local), local)

    rows = local // LY
    tall = LY + ROW_PAD

    def span(x):
        start = x * tall
        return pl.ds(pl.multiple_of(start, 8) if ROW_PAD % 8 == 0 else start, LY)

    for mask in range(parts):
        for row in range(rows):
            work[span(partner(parts, mask) * rows + row), :] = pieces[mask][row * LY : (row + 1) * LY, :]
    step = TALL // LX
    for moment in range(SLICES):

        @pl.loop(0, sites // TALL // UNROLL)
        def _(turn):
            for q in range(UNROLL):
                x = (turn * UNROLL + q) * step
                data = jnp.concatenate([work[span(x + r), :] for r in range(step)], axis=0)
                loss = loss_ref[pl.ds(pl.multiple_of(x * LY, TALL), TALL), moment : moment + 1]
                data = mix_rows(left_y_ref[...], data * loss)
                for r in range(step):
                    work[span(x + r), :] = data[r * LY : (r + 1) * LY]

        @pl.loop(0, LY // step // UNROLL)
        def _(turn):
            for r in range(UNROLL):
                y = (turn * UNROLL + r) * step
                data = jnp.concatenate([work[pl.ds(y + q, LX, stride=tall), :] for q in range(step)], axis=0)
                data = mix_rows(left_x_ref[...], data)
                for q in range(step):
                    work[pl.ds(y + q, LX, stride=tall), :] = data[q * LX : (q + 1) * LX]

    for mask in range(parts):
        for row in range(rows):
            outs[mask][row * LY : (row + 1) * LY, :] = work[span(partner(parts, mask) * rows + row), :]


def right_chain(parts, loss, left_y, left_x, pieces):
    sites = loss.shape[0]
    whole = lambda array: pl.BlockSpec(array.shape, lambda g: (0,) * array.ndim)
    return pl.pallas_call(
        functools.partial(right_body, parts),
        grid=(1,),
        in_specs=[whole(loss), whole(left_y), whole(left_x)] + [whole(piece) for piece in pieces],
        out_specs=[whole(piece) for piece in pieces],
        out_shape=[jax.ShapeDtypeStruct(piece.shape, F32) for piece in pieces],
        scratch_shapes=[pltpu.VMEM(((sites // LY + 1) * (LY + ROW_PAD), LANES), F32)],
        compiler_params=pltpu.CompilerParams(vmem_limit_bytes=RIGHT_LIMIT),
        cost_estimate=pl.CostEstimate(flops=sites * LANES * 256 * 2 * 6, bytes_accessed=sites * LANES * 12, transcendentals=0),
        name="right_chain",
    )(loss, left_y, left_x, *pieces)


def place_body(parts, lane, held, *rest):
    blocks, out, sems = rest[:parts], rest[parts + held], rest[-1]
    local = out.shape[1] // parts
    copies = []
    for mask in range(parts):
        start = pl.multiple_of(partner(parts, mask) * local + lane, LANES)
        copies.append(pltpu.make_async_copy(blocks[mask], out.at[:, pl.ds(start, LANES)], sems.at[mask]))
    for copy in copies:
        copy.start()
    for copy in copies:
        copy.wait()


def place(parts, lane, blocks, held=None):
    rows = blocks[0].shape[0]
    held = [] if held is None else [held]
    anywhere = pl.BlockSpec(memory_space=pl.ANY)
    return pl.pallas_call(
        functools.partial(place_body, parts, lane, len(held)),
        in_specs=[pl.BlockSpec(memory_space=pltpu.VMEM)] * parts + [anywhere] * len(held),
        out_specs=anywhere,
        out_shape=jax.ShapeDtypeStruct((rows, rows * parts), F32),
        scratch_shapes=[pltpu.SemaphoreType.DMA((parts,))],
        input_output_aliases={parts: 0} if held else {},
        compiler_params=pltpu.CompilerParams(vmem_limit_bytes=PLACE_LIMIT),
        cost_estimate=pl.CostEstimate(flops=0, bytes_accessed=rows * LANES * parts * 8, transcendentals=0),
        name="place",
    )(*blocks, *held)


def kernel(length, growth):
    indices = jnp.arange(length, dtype=jnp.int32)
    phases = indices[:, None] * indices[None, :] % length
    angles = 2.0 * jnp.pi * phases.astype(jnp.float32) / length
    cosines = jnp.cos(angles)
    sines = jnp.sin(angles)
    spectrum = jnp.exp(growth * jnp.cos(2.0 * jnp.pi * indices.astype(jnp.float32) / length))
    highest = lax.Precision.HIGHEST
    total = jnp.dot(cosines * spectrum[None, :], cosines.T, precision=highest)
    total = total + jnp.dot(sines * spectrum[None, :], sines.T, precision=highest)
    return total / length


def whole_exchange(green_by_column, field):
    highest = lax.Precision.HIGHEST
    walkers, local_cols, sites = green_by_column.shape
    fwd_x = kernel(LX, hop_rate)
    fwd_y = kernel(LY, hop_rate)
    inv_x = kernel(LX, -hop_rate)
    inv_y = kernel(LY, -hop_rate)
    spins = 2.0 * field.astype(jnp.float32) - 1.0
    green = green_by_column
    for moment in range(SLICES):
        left_green = green
        left_green = left_green * jnp.exp(coupling * spins[:, moment, :])[:, None, :]
        left_blocks = left_green.reshape(walkers, local_cols, LX, LY)
        left_blocks = jnp.einsum("xa,wcab->wcxb", fwd_x, left_blocks, precision=highest)
        left_blocks = jnp.einsum("yb,wcxb->wcxy", fwd_y, left_blocks, precision=highest)
        green = left_blocks.reshape(walkers, local_cols, sites)
    parts = lax.axis_size("cols")
    shaped_in = green.reshape(walkers, local_cols, parts, sites // parts)
    row_block = lax.all_to_all(shaped_in, "cols", split_axis=2, concat_axis=1, tiled=True)
    count = row_block.shape[0]
    width = row_block.shape[3]
    blocks = row_block.reshape(count, sites, width)
    for moment in range(SLICES):
        blocks = blocks * jnp.exp(-coupling * spins[:, moment, :])[:, :, None]
        shaped = blocks.reshape(count, LX, LY, width)
        shaped = jnp.einsum("by,wabr->wayr", inv_y, shaped, precision=highest)
        shaped = jnp.einsum("ax,wayr->wxyr", inv_x, shaped, precision=highest)
        blocks = shaped.reshape(count, sites, width)
    rows_done = blocks.reshape(count, sites, 1, width)
    rows_done = rows_done.reshape(walkers, sites, sites // parts)
    green = lax.all_to_all(rows_done, "cols", split_axis=1, concat_axis=2, tiled=True)
    return green


class Links:
    def __init__(self, parts):
        self.parts = parts
        self.sent = []
        self.after = None

    def send(self, block, mask):
        hold = [self.after] if self.after is not None else []
        back = len(self.sent) - IN_FLIGHT
        if back >= 0:
            hold.append(self.sent[back]["value"])
        if hold:
            got = lax.optimization_barrier(tuple([block] + hold))
            block = got[0]
            if back >= 0:
                self.sent[back]["value"] = got[-1]
        value = lax.ppermute(block, "cols", [(s, s ^ mask) for s in range(self.parts)])
        self.sent.append({"value": value})
        return self.sent[-1]


def send_order(parts, pattern):
    far = [m for pair in zip(range(3 * parts // 4, parts), range(parts // 2, 3 * parts // 4)) for m in pair]
    near = [m for pair in zip(range(parts // 4, parts // 2), range(1, parts // 4 + 1)) for m in pair][: parts // 2 - 1]
    order = []
    for kind in pattern:
        side = far if kind == "f" else near
        if side:
            order.append(side.pop(0))
    return order + near + far


def pipelined(green_by_column, field):
    _, rows, sites = green_by_column.shape
    parts = lax.axis_size("cols")
    x = green_by_column.reshape(rows, sites)
    (fwd_x, fwd_x_factor), (fwd_y, fwd_y_factor) = steady(circulant(LX, hop_rate)), steady(circulant(LY, hop_rate))
    (inv_x, inv_x_factor), (inv_y, inv_y_factor) = steady(circulant(LX, -hop_rate)), steady(circulant(LY, -hop_rate))
    loss = jnp.exp(-coupling * (2.0 * field[0].astype(F32) - 1.0)).T / (inv_x_factor * inv_y_factor)
    shrink = 1.0 / (fwd_x_factor * fwd_y_factor)
    right, left, left_y, left_x = lane_side(fwd_y), row_side(fwd_x), row_side(inv_y), row_side(inv_x)
    links = Links(parts)

    def chain(pieces):
        return right_chain(parts, loss, left_y, left_x, [pieces[mask]["value"] for mask in range(parts)])

    halves_ = left_chain(parts, shrink, rows // 4, x, field.transpose(1, 0, 2), right, left)
    sent = [{0: {"value": blocks[0]}} for blocks in halves_]
    done = []
    for h in range(2):
        for at, mask in enumerate(send_order(parts, PATTERNS[h])):
            if h == 1 and at == LATE:
                done.append(chain(sent[0]))
                links.after = done[0][0]
            sent[h][mask] = links.send(halves_[h][mask], mask)
    back = []
    for h in range(2):
        back.append({0: {"value": done[h][0]}})
        for at, mask in enumerate(send_order(parts, PATTERNS[2 + h])):
            if h == 0 and at == AHEAD:
                done.append(chain(sent[1]))
                links.after = done[1][0]
            back[h][mask] = links.send(done[h][mask], mask)
    result = None
    for h in range(2):
        result = place(parts, h * LANES, [back[h][mask]["value"] for mask in range(parts)], result)
    return result.reshape(green_by_column.shape)


def shards(green_by_column, field):
    walkers, rows, sites = green_by_column.shape
    parts = lax.axis_size("cols")
    fits = walkers == 1 and rows == 256 and rows * parts == sites and parts & (parts - 1) == 0 and parts >= 8
    if fits and LX * LY == sites and LX == LY == 64:
        return pipelined(green_by_column, field)
    return whole_exchange(green_by_column, field)


def solution(mesh):
    return jax.shard_map(
        shards,
        mesh=mesh,
        in_specs=(P("walk", "cols", None), P("walk", None, None)),
        out_specs=P("walk", "cols", None),
        check_vma=False,
    )
```
